32 devices in a mesh: dp: 32 (over z, y, x, core), ctx: 1.
Axes of the slice: x: 2, y: 2, z: 4, core: 2. Of those that a mesh axis runs over, the one named last changes fastest.
Arguments:
- query: bfloat16 [32, 128, 4096], P('dp', 'ctx'), may hold values from -128 to 128
- key: bfloat16 [32, 128, 1024], P('dp', 'ctx'), may hold values from -6 to 6
- value: bfloat16 [32, 128, 1024], P('dp', 'ctx'), may hold values from -6 to 6
- gate_input: bfloat16 [32, 128, 4096], P('dp', 'ctx'), may hold values from -6 to 6
- conv_weight: bfloat16 [4, 4096], P(None, 'dp'), may hold values from -3 to 3
- conv_bias: bfloat16 [4096], P('dp'), may hold values from -3 to 3
- x_proj: bfloat16 [4096, 288], P('dp'), may hold values from -0.375 to 0.375
- dt_proj: bfloat16 [256, 4096], P(None, 'dp'), may hold values from -0.375 to 0.375
- dt_bias: bfloat16 [4096], P('dp'), may hold values from -7 to -2.296875
- a_log: bfloat16 [16, 4096], P(None, 'dp'), may hold values from 0 to 2.765625
- d_skip: bfloat16 [4096], P('dp'), may hold values from 0.19921875 to 1
- out_proj: bfloat16 [4096, 2048], P('dp'), may hold values from -0.09375 to 0.09375
Outputs:
- result: bfloat16 [32, 128, 2048], P('dp', 'ctx')
The draws below stay inside these ranges and needn't reach their ends.
All inputs are finite; a program needn't handle non-finite values.
Results may differ from the reference program's by a relative error of at most 0.008.
Values may be sent and summed in bfloat16 or wider, within the bound.
No kernel may reach another device: no remote copies, remote signals or barrier semaphores. Data moves between devices by JAX's collectives and lax.ppermute only.
A program may use at most 128 MiB of HBM per device.

```python
import math
import jax
import jax.numpy as jnp
from jax import lax

QUERY_HEADS = 32
KEY_VALUE_HEADS = 8
HEAD_SIZE = 128
DM = 2048
NS = 16
RANK = 256
KC = 4
E = 4096
SEQUENCE_LENGTH = 128
SEQUENCE_COUNT = 32


def pairing(key):
    base_offset = jax.random.truncated_normal(jax.random.fold_in(key, 101), -6.0, 6.0, (SEQUENCE_COUNT, SEQUENCE_LENGTH, KEY_VALUE_HEADS * HEAD_SIZE), jnp.float32)
    return base_offset


def draw_key(key, part):
    base_offset = pairing(key)
    return base_offset.astype(jnp.bfloat16)


def draw_query(key, part):
    noise = jax.random.truncated_normal(jax.random.fold_in(key, 104), -6.0, 6.0, (SEQUENCE_COUNT, SEQUENCE_LENGTH, QUERY_HEADS * HEAD_SIZE), jnp.float32)
    return noise.astype(jnp.bfloat16)


def block_levels(stream_key, dims, cuts, low, top_value):
    factor_of = 1.0
    for axis_at, blocks in cuts:
        steps = jax.random.uniform(jax.random.fold_in(jax.random.fold_in(stream_key, 6), axis_at), (blocks,), jnp.float32, low / len(cuts), top_value / len(cuts))
        factor_of = factor_of * jnp.repeat(jnp.exp(steps), dims[axis_at] // blocks).reshape((-1,) + (1,) * (len(dims) - 1 - axis_at))
    return factor_of


def bell_draw(key, shape, spread, bound, cuts=(), kind=jnp.bfloat16):
    factor_of = block_levels(key, shape, cuts, -0.22, 0.18) if cuts else 1.0
    values = jax.random.normal(key, shape, jnp.float32) * spread * factor_of
    return jnp.minimum(jnp.maximum(values, -bound), bound).astype(kind)


def setup_inputs(seed: int = 0) -> dict:
    arg_keys = jax.random.split(jax.random.key(seed), 13)
    query = draw_query(jax.random.fold_in(arg_keys[12], 71), 0)
    key = draw_key(jax.random.fold_in(arg_keys[12], 71), 0)
    value = bell_draw(arg_keys[2], (SEQUENCE_COUNT, SEQUENCE_LENGTH, KEY_VALUE_HEADS * HEAD_SIZE), 1.0, 6.0, ((0, 32),))
    gate_input = bell_draw(arg_keys[3], (SEQUENCE_COUNT, SEQUENCE_LENGTH, E), 1.0, 6.0, ((0, 32),))
    conv_weight = bell_draw(arg_keys[4], (KC, E), KC ** -0.5, 3.0, ((1, 32),))
    conv_bias = bell_draw(arg_keys[5], (E,), 0.5, 3.0, ((0, 32),))
    x_proj = bell_draw(arg_keys[6], (E, RANK + 2 * NS), (E // 16) ** -0.5, 0.375, ((0, 32),))
    dt_proj = bell_draw(arg_keys[7], (RANK, E), RANK ** -0.5, 0.375, ((1, 32),))
    dt_bias = jnp.clip(-7.0 + 4.703125 * jax.random.uniform(arg_keys[8], (E,), jnp.float32) ** block_levels(arg_keys[8], (E,), ((0, 32),), -0.2, 0.2), -7.0, -2.296875).astype(jnp.bfloat16)
    a_log = jnp.clip(2.765625 * jax.random.uniform(arg_keys[9], (NS, E), jnp.float32) ** block_levels(arg_keys[9], (NS, E), ((1, 32),), -0.2, 0.2), 0.0, 2.765625).astype(jnp.bfloat16)
    d_skip = jnp.clip(0.19921875 + 0.80078125 * jax.random.uniform(arg_keys[10], (E,), jnp.float32) ** block_levels(arg_keys[10], (E,), ((0, 32),), -0.2, 0.2), 0.19921875, 1.0).astype(jnp.bfloat16)
    out_proj = bell_draw(arg_keys[11], (E, DM), E ** -0.5, 0.09375, ((0, 32),))
    return {"query": query, "key": key, "value": value, "gate_input": gate_input, "conv_weight": conv_weight, "conv_bias": conv_bias, "x_proj": x_proj, "dt_proj": dt_proj, "dt_bias": dt_bias, "a_log": a_log, "d_skip": d_skip, "out_proj": out_proj}


def attend(query_rows, key_rows, value_rows):
    seq_len = query_rows.shape[0]
    heads = query_rows.shape[1] // HEAD_SIZE
    kv_heads = key_rows.shape[1] // HEAD_SIZE
    group = heads // kv_heads
    scale = 1.0 / math.sqrt(HEAD_SIZE)
    queries = query_rows.reshape(seq_len, kv_heads, group, HEAD_SIZE).astype(jnp.float32)
    keys_all = key_rows.reshape(seq_len, kv_heads, HEAD_SIZE).astype(jnp.float32)
    values_all = value_rows.reshape(seq_len, kv_heads, HEAD_SIZE).astype(jnp.float32)
    block = min(512, seq_len)
    pieces = []
    for index in range(seq_len // block):
        begin = index * block
        end = begin + block
        scores = jnp.einsum('rgqd,ngd->gqrn', queries[begin:end], keys_all[:end]) * scale
        visible = jnp.arange(end)[None, :] <= (begin + jnp.arange(block))[:, None]
        scores = jnp.where(visible, scores, -jnp.inf)
        top = lax.optimization_barrier(jnp.max(scores, axis=-1, keepdims=True))
        raised = jnp.exp(scores - top)
        total = lax.optimization_barrier(jnp.sum(raised, axis=-1))
        weights = lax.optimization_barrier(raised.astype(jnp.bfloat16)).astype(jnp.float32)
        mixed = jnp.einsum('gqrn,ngd->rgqd', weights, values_all[:end])
        mixed = mixed / jnp.transpose(total, (2, 0, 1))[..., None]
        pieces.append(mixed.astype(jnp.bfloat16).reshape(block, heads * HEAD_SIZE))
    return lax.optimization_barrier(jnp.concatenate(pieces, axis=0))

def scan_layer(mixed, gate_rows, conv_weight, conv_bias, x_proj, dt_proj, dt_bias, a_log, d_skip, out_proj):
    seq_len, channels = mixed.shape
    taps = conv_weight.shape[0]
    padded = jnp.concatenate([jnp.zeros((taps - 1, channels), jnp.float32), mixed.astype(jnp.float32)], axis=0)
    filtered = conv_bias.astype(jnp.float32)[None, :]
    for tap in range(taps):
        filtered = filtered + conv_weight[tap].astype(jnp.float32)[None, :] * padded[tap:tap + seq_len]
    smoothed = lax.optimization_barrier(jax.nn.silu(filtered).astype(jnp.bfloat16))
    projected = jnp.dot(smoothed, x_proj, preferred_element_type=jnp.float32)
    low_rank = projected[:, :RANK]
    normed = (low_rank * lax.rsqrt(lax.optimization_barrier(jnp.mean(low_rank * low_rank, axis=-1, keepdims=True)) + 1e-06)).astype(jnp.bfloat16)
    step_size = jax.nn.softplus(jnp.dot(normed, dt_proj, preferred_element_type=jnp.float32) + dt_bias.astype(jnp.float32)[None, :])
    input_gain = projected[:, RANK:RANK + NS]
    readout = projected[:, RANK + NS:RANK + 2 * NS]
    decay_rate = -jnp.exp(a_log.astype(jnp.float32))
    smooth_float = smoothed.astype(jnp.float32)
    drive_term = step_size * smooth_float

    def advance(state, inputs):
        size_row, drive_row, gain_row, read_row = inputs
        state = jnp.exp(size_row[None, :] * decay_rate) * state + gain_row[:, None] * drive_row[None, :]
        return (state, jnp.dot(read_row, state, precision=lax.Precision.HIGHEST))
    initial = jnp.zeros((NS, channels), jnp.float32)
    _, scanned = lax.scan(advance, initial, (step_size, drive_term, input_gain, readout))
    scan_out = scanned + d_skip.astype(jnp.float32)[None, :] * smooth_float
    gated = (scan_out * jax.nn.silu(gate_rows.astype(jnp.float32))).astype(jnp.bfloat16)
    return jnp.dot(gated, out_proj, preferred_element_type=jnp.float32).astype(jnp.bfloat16)

def reference(query, key, value, gate_input, conv_weight, conv_bias, x_proj, dt_proj, dt_bias, a_log, d_skip, out_proj):

    def one_sequence(items):
        query_rows, key_rows, value_rows, gate_rows = items
        mixed = attend(query_rows, key_rows, value_rows)
        return scan_layer(mixed, gate_rows, conv_weight, conv_bias, x_proj, dt_proj, dt_bias, a_log, d_skip, out_proj)
    return lax.map(one_sequence, (query, key, value, gate_input))
```

```python
import functools
import math

import jax
import jax.numpy as jnp
from jax import lax
from jax.experimental import pallas as pl
from jax.experimental.pallas import tpu as pltpu
from jax.sharding import PartitionSpec as P

HEAD_SIZE = 128


def shifted(value, axis, steps):
    count = lax.axis_size(axis)
    initial, last = (max(0, -steps), min(count, count - steps))
    return lax.ppermute(value, axis, [(source, source + steps) for source in range(initial, last)])


def entering(shard, axis, combine, identity):
    size, position = (lax.axis_size(axis), lax.axis_index(axis))
    everything = jax.tree.map(lambda part: lax.all_gather(part, axis), shard)
    start = jax.tree.map(
        lambda part, zero: jnp.broadcast_to(jnp.asarray(zero, part.dtype), part.shape),
        shard,
        identity,
    )

    def hop(k, before):
        reached = k < position
        new = combine(before, jax.tree.map(lambda part: part[k], everything))
        return jax.tree.map(lambda a, b: jnp.where(reached, a, b), new, before)

    return lax.fori_loop(0, size, hop, start)


def attend_whole(queries, keys_all, values_all, group):
    seq_len, kv_local, head_dim = keys_all.shape
    scale = 1.0 / math.sqrt(head_dim)
    block = min(512, seq_len)
    pieces = []
    for index in range(seq_len // block):
        begin = index * block
        end = begin + block
        query_block = queries[begin:end].reshape(block, kv_local, group, head_dim)
        scores = (
            jnp.einsum(
                "rgqd,ngd->gqrn", query_block, keys_all[:end], preferred_element_type=jnp.float32
            )
            * scale
        )
        visible = jnp.arange(end)[None, :] <= (begin + jnp.arange(block))[:, None]
        scores = jnp.where(visible, scores, -jnp.inf)
        top = jnp.max(scores, axis=-1, keepdims=True)
        raised = jnp.exp(scores - top)
        total = jnp.sum(raised, axis=-1)
        mixed = jnp.einsum(
            "gqrn,ngd->rgqd",
            raised.astype(jnp.bfloat16),
            values_all[:end],
            preferred_element_type=jnp.float32,
        )
        mixed = mixed / jnp.transpose(total, (2, 0, 1))[..., None]
        pieces.append(mixed.astype(jnp.bfloat16).reshape(block, kv_local, group * head_dim))
    return jnp.concatenate(pieces, axis=0)


def chain_pass(initial, step_size, drive_term, input_gain, readout, decay_rate):
    tok_rows = step_size.shape[0]
    block_len = math.gcd(tok_rows, 32)
    blocks = tok_rows // block_len

    def advance(state, inputs):
        size_block, drive_block, gain_block, read_block = inputs
        outputs = []
        for position in range(block_len):
            state = jnp.exp(size_block[position][None, :] * decay_rate) * state
            state = state + gain_block[position][:, None] * drive_block[position][None, :]
            outputs.append(jnp.dot(read_block[position], state, precision=lax.Precision.HIGHEST))
        return (state, jnp.stack(outputs))

    inputs = tuple(
        (
            item.reshape((blocks, block_len) + item.shape[1:])
            for item in (step_size, drive_term, input_gain, readout)
        )
    )
    final, outputs = lax.scan(advance, initial, inputs)
    return (final, outputs.reshape(tok_rows, -1))


def carried_part(carried, step_size, readout, decay_rate):
    tok_rows, channels = step_size.shape
    lower = (jnp.arange(tok_rows)[:, None] >= jnp.arange(tok_rows)[None, :]).astype(jnp.float32)
    cumulative = jnp.dot(lower, step_size, precision=lax.Precision.HIGHEST)
    block_len = math.gcd(tok_rows, 32)
    blocks = tok_rows // block_len
    cum_blocks = cumulative.reshape(blocks, block_len, channels)
    read_blocks = readout.reshape(blocks, block_len, readout.shape[1])

    def one_block(items):
        cum_block, read_block = items
        factor = jnp.exp(cum_block[:, None, :] * decay_rate[None])
        return jnp.sum(read_block[:, :, None] * factor * carried[None], axis=1)

    return lax.map(one_block, (cum_blocks, read_blocks)).reshape(tok_rows, channels)


def shards(
    query,
    key,
    value,
    gate_input,
    conv_weight,
    conv_bias,
    x_proj,
    dt_proj,
    dt_bias,
    a_log,
    d_skip,
    out_proj,
):
    tok_rows = query.shape[1]
    feature_width = query.shape[2]
    head_dim = HEAD_SIZE
    kv_heads = key.shape[2] // head_dim
    group = feature_width // key.shape[2]
    queries = query[0].reshape(tok_rows, kv_heads, group * head_dim)
    key_rows = key[0].reshape(tok_rows, kv_heads, head_dim)
    value_rows = value[0].reshape(tok_rows, kv_heads, head_dim)
    gathered_queries, gathered_keys, gathered_values = (
        lax.all_to_all(queries, "ctx", split_axis=1, concat_axis=0, tiled=True),
        lax.all_to_all(key_rows, "ctx", split_axis=1, concat_axis=0, tiled=True),
        lax.all_to_all(value_rows, "ctx", split_axis=1, concat_axis=0, tiled=True),
    )
    mixed = lax.all_to_all(
        attend_whole(gathered_queries, gathered_keys, gathered_values, group),
        "ctx",
        split_axis=0,
        concat_axis=1,
        tiled=True,
    )
    layer_input = mixed.reshape(tok_rows, feature_width)
    filter_taps, filter_bias, input_weight, step_weight, step_bias, decay_log, skip_gain = (
        lax.all_gather(conv_weight, "dp", axis=1, tiled=True),
        lax.all_gather(conv_bias, "dp", axis=0, tiled=True),
        lax.all_gather(x_proj, "dp", axis=0, tiled=True),
        lax.all_gather(dt_proj, "dp", axis=1, tiled=True),
        lax.all_gather(dt_bias, "dp", axis=0, tiled=True),
        lax.all_gather(a_log, "dp", axis=1, tiled=True),
        lax.all_gather(d_skip, "dp", axis=0, tiled=True),
    )
    taps = filter_taps.shape[0]
    earlier = shifted(layer_input[tok_rows - (taps - 1) :], "ctx", 1)
    padded = jnp.concatenate([earlier, layer_input], axis=0).astype(jnp.float32)
    filtered = filter_bias.astype(jnp.float32)[None, :]
    for tap in range(taps):
        filtered = (
            filtered + filter_taps[tap].astype(jnp.float32)[None, :] * padded[tap : tap + tok_rows]
        )
    smoothed = jax.nn.silu(filtered).astype(jnp.bfloat16)
    projected = jnp.dot(smoothed, input_weight, preferred_element_type=jnp.float32)
    rank = step_weight.shape[0]
    states = decay_log.shape[0]
    low_rank = projected[:, :rank]
    normed = (
        low_rank * lax.rsqrt(jnp.mean(low_rank * low_rank, axis=-1, keepdims=True) + 1e-06)
    ).astype(jnp.bfloat16)
    step_size = jax.nn.softplus(
        jnp.dot(normed, step_weight, preferred_element_type=jnp.float32)
        + step_bias.astype(jnp.float32)[None, :]
    )
    input_gain = projected[:, rank : rank + states]
    readout = projected[:, rank + states : rank + 2 * states]
    decay_rate = -jnp.exp(decay_log.astype(jnp.float32))
    smooth_float = smoothed.astype(jnp.float32)
    drive_term = step_size * smooth_float
    empty_state = jnp.zeros((states, feature_width), jnp.float32)
    end_state, local_out = chain_pass(
        empty_state, step_size, drive_term, input_gain, readout, decay_rate
    )
    total_decay = jnp.exp(decay_rate * jnp.sum(step_size, axis=0)[None, :])

    def combine(earlier_pair, later_pair):
        return (earlier_pair[0] * later_pair[0], later_pair[0] * earlier_pair[1] + later_pair[1])

    _, carried = entering(
        (total_decay, end_state),
        "ctx",
        combine,
        (jnp.ones_like(total_decay), jnp.zeros_like(end_state)),
    )
    carried_out = carried_part(carried, step_size, readout, decay_rate)
    scan_out = local_out + carried_out + skip_gain.astype(jnp.float32)[None, :] * smooth_float
    gated = (scan_out * jax.nn.silu(gate_input[0].astype(jnp.float32))).astype(jnp.bfloat16)
    piece = lax.all_gather(out_proj, "dp", axis=0, tiled=True)
    columns = lax.slice_in_dim(gated, 0, piece.shape[0], axis=1)
    result = jnp.zeros((tok_rows, out_proj.shape[1]), jnp.float32) + jnp.dot(
        columns, piece, preferred_element_type=jnp.float32
    )
    return result.astype(jnp.bfloat16)[None]


HEAD = HEAD_SIZE
RANK = 256
STATES = 16
TAPS = 4
EPS = 1e-06
LOG2E = 1.4426950408889634
GROUP = 4
XW, DT, AL, MISC, PACK_ROWS = 0, 288, 544, 560, 576


def swap(value, distance, count):
    return lax.ppermute(value, "dp", [(i, i ^ distance) for i in range(count)])


def local_call(kernel, out_shape, name, scratch=(), flops=0, bytes_accessed=0, transcendentals=0):
    def call(*args):
        return pl.pallas_call(
            kernel,
            out_shape=out_shape,
            in_specs=[pl.BlockSpec(memory_space=pltpu.VMEM)] * len(args),
            out_specs=jax.tree.map(lambda _: pl.BlockSpec(memory_space=pltpu.VMEM), out_shape),
            scratch_shapes=list(scratch),
            name=name,
            cost_estimate=pl.CostEstimate(
                flops=flops, bytes_accessed=bytes_accessed, transcendentals=transcendentals
            ),
            compiler_params=pltpu.CompilerParams(vmem_limit_bytes=48 * 1024 * 1024),
        )(*args)

    return call


def attention_kernel(q_ref, k_ref, v_ref, g_ref, keep_ref, send_ref, gkeep_ref, gsend_ref):
    position = lax.axis_index("dp")
    member, block = position % GROUP, position // GROUP
    rows = q_ref.shape[0]
    scale = 1.0 / math.sqrt(HEAD)
    row = lax.broadcasted_iota(jnp.int32, (GROUP, rows, rows), 1).reshape(GROUP * rows, rows)
    col = lax.broadcasted_iota(jnp.int32, (GROUP * rows, rows), 1)
    visible = col <= row

    def lanes(index):
        return pl.ds(pl.multiple_of(index * HEAD, HEAD), HEAD)

    for slot in range(8):
        kv = block ^ slot
        heads = [kv * GROUP + (member ^ j) for j in range(GROUP)]
        stacked = jnp.concatenate([q_ref[:, lanes(h)] for h in heads], axis=0)
        keys = k_ref[:, lanes(kv)]
        values = v_ref[:, lanes(kv)]
        scores = lax.dot_general(
            stacked, keys, (((1,), (1,)), ((), ())), preferred_element_type=jnp.float32
        )
        scores = jnp.where(visible, scores * scale, -jnp.inf)
        top = jnp.max(scores, axis=-1, keepdims=True)
        raised = jnp.exp(scores - top)
        total = jnp.sum(raised, axis=-1, keepdims=True)
        mixed = jnp.dot(raised.astype(jnp.bfloat16), values, preferred_element_type=jnp.float32)
        mixed = (mixed / total).astype(jnp.bfloat16)
        here = slice(slot * HEAD, (slot + 1) * HEAD)
        for j in range(GROUP):
            target = send_ref if j % 2 else keep_ref
            gtarget = gsend_ref if j % 2 else gkeep_ref
            target[j // 2, :, here] = mixed[j * rows : (j + 1) * rows]
            gtarget[j // 2, :, here] = g_ref[:, lanes(heads[j])]


def project_kernel(*refs):
    packs, (keep_ref, recv_ref, x1_ref, x2_ref), rest = refs[:8], refs[8:12], refs[12:]
    smooth_ref, pkeep_ref, psend_ref, weight_ref = rest
    rows = keep_ref.shape[1]
    row = lax.broadcasted_iota(jnp.int32, (rows, HEAD), 0)
    masks = [row >= k for k in range(TAPS)]
    sources = [keep_ref.at[0], recv_ref.at[0], x1_ref.at[0], x2_ref.at[0]]
    for slot in range(8):
        here = slice(slot * HEAD, (slot + 1) * HEAD)
        weight_ref[:, here] = packs[slot][XW : XW + 288, :]
        misc = packs[slot][MISC : MISC + 16, :].astype(jnp.float32)
        for j in range(GROUP):
            mixed = sources[j][:, here].astype(jnp.float32)
            filtered = misc[4:5] + jnp.zeros_like(mixed)
            for tap in range(TAPS):
                shift = TAPS - 1 - tap
                moved = mixed
                if shift:
                    moved = jnp.where(masks[shift], pltpu.roll(mixed, shift, 0), 0.0)
                filtered = filtered + misc[tap : tap + 1] * moved
            smooth = filtered / (1.0 + jnp.exp(-filtered))
            smooth_ref[j, :, here] = smooth.astype(jnp.bfloat16)
    for j in range(GROUP):
        part = lax.dot_general(
            smooth_ref[j],
            weight_ref[...],
            (((1,), (1,)), ((), ())),
            preferred_element_type=jnp.float32,
        )
        target = psend_ref if j % 2 else pkeep_ref
        half = j // 2
        target[:, half * 256 : half * 256 + 256] = part[:, :256]
        target[:, 512 + half * 32 : 512 + half * 32 + 32] = part[:, 256:288]


def scan_kernel(half, *refs):
    packs, (f0_ref, f1_ref, smooth_ref, ga_ref, gb_ref), rest = refs[:8], refs[8:13], refs[13:]
    gated_ref, size_ref, drive_ref, out_ref, rate_ref, gain_ref, read_ref = rest
    rows = f0_ref.shape[0]
    sources = [f0_ref, f1_ref]
    gates = [ga_ref, gb_ref]
    for s in range(2):
        low = sources[s][:, half * 256 : half * 256 + 256]
        normed = low * lax.rsqrt(jnp.mean(low * low, axis=-1, keepdims=True) + EPS)
        normed = normed.astype(jnp.bfloat16)
        both = sources[s][:, 512 + half * 32 : 512 + half * 32 + 32]
        for n in range(STATES):
            wide = jnp.broadcast_to(both[:, n : n + 1], (rows, HEAD))
            gain_ref[s, pl.ds(n, rows, stride=STATES), :] = wide
            wide = jnp.broadcast_to(both[:, STATES + n : STATES + n + 1], (rows, HEAD))
            read_ref[s, pl.ds(n, rows, stride=STATES), :] = wide
        for slot in range(8):
            bias = packs[slot][MISC : MISC + 16, :].astype(jnp.float32)[5:6]
            raw = (
                jnp.dot(
                    normed, packs[slot][DT : DT + RANK, :], preferred_element_type=jnp.float32
                )
                + bias
            )
            size = jnp.maximum(raw, 0.0) + jnp.log1p(jnp.exp(-jnp.abs(raw)))
            smooth = smooth_ref[2 * half + s, :, slot * HEAD : (slot + 1) * HEAD]
            size_ref[s, pl.ds(slot, rows, stride=8), :] = size
            drive_ref[s, pl.ds(slot, rows, stride=8), :] = size * smooth.astype(jnp.float32)
    for slot in range(8):
        rate = -jnp.exp(packs[slot][AL : AL + STATES, :].astype(jnp.float32)) * LOG2E
        rate_ref[pl.ds(slot, STATES, stride=8), :] = rate

    def one(t, states):
        new = []
        for s in range(2):
            at = pl.ds(pl.multiple_of(t * 8, 8), 8)
            size = size_ref[s, at, :]
            drive = drive_ref[s, at, :]
            total = [None, None]
            for n in range(STATES):
                decay = jnp.exp2(size * rate_ref[n * 8 : n * 8 + 8, :])
                gain = gain_ref[s, pl.ds(t * STATES + n, 1), :]
                read = read_ref[s, pl.ds(t * STATES + n, 1), :]
                state = decay * states[s * STATES + n] + gain * drive
                new.append(state)
                term = read * state
                total[n % 2] = term if total[n % 2] is None else total[n % 2] + term
            out_ref[s, at, :] = total[0] + total[1]
        return tuple(new)

    zero = jnp.zeros((8, HEAD), jnp.float32)
    lax.fori_loop(0, rows, one, (zero,) * (2 * STATES), unroll=2)
    for s in range(2):
        for slot in range(8):
            here = slice(slot * HEAD, (slot + 1) * HEAD)
            skip = packs[slot][MISC : MISC + 16, :].astype(jnp.float32)[6:7]
            smooth = smooth_ref[2 * half + s, :, here].astype(jnp.float32)
            scanned = out_ref[s, pl.ds(slot, rows, stride=8), :] + skip * smooth
            gate = gates[s][0, :, here].astype(jnp.float32)
            gated = scanned * (gate / (1.0 + jnp.exp(-gate)))
            gated_ref[s * rows : (s + 1) * rows, here] = gated.astype(jnp.bfloat16)


def output_kernel(*refs):
    slots, gated_ref, (keep_ref, send_ref) = refs[:8], refs[8], refs[9:]
    rows = keep_ref.shape[0]
    width = 512
    for begin in range(0, keep_ref.shape[1], width):
        columns = slice(begin, begin + width)
        weight = jnp.concatenate([slots[slot][:, columns] for slot in range(8)], axis=0)
        total = jnp.dot(gated_ref[...], weight, preferred_element_type=jnp.float32)
        keep_ref[:, columns] = total[:rows]
        send_ref[:, columns] = total[rows:].astype(send_ref.dtype)


def grouped(query, key, value, gate_input, conv_weight, conv_bias, x_proj, dt_proj, dt_bias, a_log, d_skip, out_proj):
    count = lax.axis_size("dp")
    rows = query.shape[1]
    width = out_proj.shape[1]
    pack = jnp.concatenate(
        [
            x_proj.T,
            dt_proj,
            a_log,
            conv_weight,
            conv_bias[None],
            dt_bias[None],
            d_skip[None],
            jnp.zeros((PACK_ROWS - MISC - 7, HEAD), jnp.bfloat16),
        ],
        axis=0,
    )

    def gathered(own):
        slots = [None] * 8
        slots[0] = own
        for even in (2, 4, 6):
            slots[even] = swap(own, GROUP * even, count)
        for even in (0, 2, 4, 6):
            slots[even + 1] = swap(slots[even], GROUP, count)
        return slots

    packs = gathered(pack)
    half = jax.ShapeDtypeStruct((2, rows, 8 * HEAD), jnp.bfloat16)
    keep, send, gkeep, gsend = local_call(
        attention_kernel, (half,) * 4, "attention",
        flops=4 * 32 * rows * rows * HEAD, bytes_accessed=6 << 20, transcendentals=32 * rows * rows,
    )(query[0], key[0], value[0], gate_input[0])
    x1 = swap(keep[1:2], 2, count)
    recv = swap(send, 1, count)
    x2 = swap(recv[1:2], 2, count)
    grecv = swap(gsend, 1, count)
    gx1 = swap(gkeep[1:2], 2, count)
    gx2 = swap(grecv[1:2], 2, count)
    slots = gathered(out_proj)
    wide = jax.ShapeDtypeStruct((rows, 640), jnp.float32)
    smooth, pkeep, psend = local_call(
        project_kernel,
        (jax.ShapeDtypeStruct((GROUP, rows, 8 * HEAD), jnp.bfloat16), wide, wide),
        "project",
        scratch=[pltpu.VMEM((288, 8 * HEAD), jnp.bfloat16)],
        flops=2 * GROUP * rows * 1024 * 288, bytes_accessed=4 << 20, transcendentals=GROUP * rows * 1024,
    )(*packs, keep, recv, x1, x2)
    chip = pkeep + swap(psend, 1, count)
    other = swap(chip, 2, count)
    other = jnp.concatenate(
        [other[:, 256:512], other[:, :256], other[:, 544:576], other[:, 512:544], other[:, 576:]],
        axis=1,
    )
    full = chip + other
    partner = swap(full, 1, count)

    def scanned(which, gate_a, gate_b):
        return local_call(
            functools.partial(scan_kernel, which),
            jax.ShapeDtypeStruct((2 * rows, 8 * HEAD), jnp.bfloat16),
            "scan",
            scratch=[
                pltpu.VMEM((2, rows * 8, HEAD), jnp.float32),
                pltpu.VMEM((2, rows * 8, HEAD), jnp.float32),
                pltpu.VMEM((2, rows * 8, HEAD), jnp.float32),
                pltpu.VMEM((STATES * 8, HEAD), jnp.float32),
                pltpu.VMEM((2, rows * STATES, HEAD), jnp.float32),
                pltpu.VMEM((2, rows * STATES, HEAD), jnp.float32),
            ],
            flops=16 * 1024 * 256 * 256, bytes_accessed=4 << 20, transcendentals=256 * 1024 * 16,
        )(*packs, full, partner, smooth, gate_a, gate_b)

    def projected_out(gated):
        return local_call(
            output_kernel,
            (
                jax.ShapeDtypeStruct((rows, width), jnp.float32),
                jax.ShapeDtypeStruct((rows, width), jnp.bfloat16),
            ),
            "output",
            flops=2 * 2 * rows * 1024 * width, bytes_accessed=6 << 20,
        )(*slots, gated)

    far_keep, far_send = projected_out(scanned(1, gx1, gx2))
    far = (far_keep + swap(far_send, 1, count).astype(jnp.float32)).astype(jnp.bfloat16)
    from_far = swap(far, 2, count)
    near_keep, near_send = projected_out(scanned(0, gkeep[0:1], grecv[0:1]))
    near = near_keep + swap(near_send, 1, count).astype(jnp.float32)
    return (near + from_far.astype(jnp.float32)).astype(jnp.bfloat16)[None]


def solution(mesh):
    placed = (
        P("dp", "ctx", None),
        P("dp", "ctx", None),
        P("dp", "ctx", None),
        P("dp", "ctx", None),
        P(None, "dp"),
        P("dp"),
        P("dp", None),
        P(None, "dp"),
        P("dp"),
        P(None, "dp"),
        P("dp"),
        P("dp", None),
    )
    fits = mesh.shape["ctx"] == 1 and mesh.shape["dp"] == 32
    return jax.shard_map(
        grouped if fits else shards, mesh=mesh, in_specs=placed, out_specs=P("dp", "ctx", None), check_vma=False
    )
```

```python
import functools
import math

import jax
import jax.numpy as jnp
from jax import lax
from jax.experimental import pallas as pl
from jax.experimental.pallas import tpu as pltpu
from jax.sharding import PartitionSpec as P

HEAD_SIZE = 128


def shifted(value, axis, steps):
    count = lax.axis_size(axis)
    initial, last = (max(0, -steps), min(count, count - steps))
    return lax.ppermute(value, axis, [(source, source + steps) for source in range(initial, last)])


def entering(shard, axis, combine, identity):
    size, position = (lax.axis_size(axis), lax.axis_index(axis))
    everything = jax.tree.map(lambda part: lax.all_gather(part, axis), shard)
    start = jax.tree.map(
        lambda part, zero: jnp.broadcast_to(jnp.asarray(zero, part.dtype), part.shape),
        shard,
        identity,
    )

    def hop(k, before):
        reached = k < position
        new = combine(before, jax.tree.map(lambda part: part[k], everything))
        return jax.tree.map(lambda a, b: jnp.where(reached, a, b), new, before)

    return lax.fori_loop(0, size, hop, start)


def attend_whole(queries, keys_all, values_all, group):
    seq_len, kv_local, head_dim = keys_all.shape
    scale = 1.0 / math.sqrt(head_dim)
    block = min(512, seq_len)
    pieces = []
    for index in range(seq_len // block):
        begin = index * block
        end = begin + block
        query_block = queries[begin:end].reshape(block, kv_local, group, head_dim)
        scores = (
            jnp.einsum(
                "rgqd,ngd->gqrn", query_block, keys_all[:end], preferred_element_type=jnp.float32
            )
            * scale
        )
        visible = jnp.arange(end)[None, :] <= (begin + jnp.arange(block))[:, None]
        scores = jnp.where(visible, scores, -jnp.inf)
        top = jnp.max(scores, axis=-1, keepdims=True)
        raised = jnp.exp(scores - top)
        total = jnp.sum(raised, axis=-1)
        mixed = jnp.einsum(
            "gqrn,ngd->rgqd",
            raised.astype(jnp.bfloat16),
            values_all[:end],
            preferred_element_type=jnp.float32,
        )
        mixed = mixed / jnp.transpose(total, (2, 0, 1))[..., None]
        pieces.append(mixed.astype(jnp.bfloat16).reshape(block, kv_local, group * head_dim))
    return jnp.concatenate(pieces, axis=0)


def chain_pass(initial, step_size, drive_term, input_gain, readout, decay_rate):
    tok_rows = step_size.shape[0]
    block_len = math.gcd(tok_rows, 32)
    blocks = tok_rows // block_len

    def advance(state, inputs):
        size_block, drive_block, gain_block, read_block = inputs
        outputs = []
        for position in range(block_len):
            state = jnp.exp(size_block[position][None, :] * decay_rate) * state
            state = state + gain_block[position][:, None] * drive_block[position][None, :]
            outputs.append(jnp.dot(read_block[position], state, precision=lax.Precision.HIGHEST))
        return (state, jnp.stack(outputs))

    inputs = tuple(
        (
            item.reshape((blocks, block_len) + item.shape[1:])
            for item in (step_size, drive_term, input_gain, readout)
        )
    )
    final, outputs = lax.scan(advance, initial, inputs)
    return (final, outputs.reshape(tok_rows, -1))


def carried_part(carried, step_size, readout, decay_rate):
    tok_rows, channels = step_size.shape
    lower = (jnp.arange(tok_rows)[:, None] >= jnp.arange(tok_rows)[None, :]).astype(jnp.float32)
    cumulative = jnp.dot(lower, step_size, precision=lax.Precision.HIGHEST)
    block_len = math.gcd(tok_rows, 32)
    blocks = tok_rows // block_len
    cum_blocks = cumulative.reshape(blocks, block_len, channels)
    read_blocks = readout.reshape(blocks, block_len, readout.shape[1])

    def one_block(items):
        cum_block, read_block = items
        factor = jnp.exp(cum_block[:, None, :] * decay_rate[None])
        return jnp.sum(read_block[:, :, None] * factor * carried[None], axis=1)

    return lax.map(one_block, (cum_blocks, read_blocks)).reshape(tok_rows, channels)


def shards(
    query,
    key,
    value,
    gate_input,
    conv_weight,
    conv_bias,
    x_proj,
    dt_proj,
    dt_bias,
    a_log,
    d_skip,
    out_proj,
):
    tok_rows = query.shape[1]
    feature_width = query.shape[2]
    head_dim = HEAD_SIZE
    kv_heads = key.shape[2] // head_dim
    group = feature_width // key.shape[2]
    queries = query[0].reshape(tok_rows, kv_heads, group * head_dim)
    key_rows = key[0].reshape(tok_rows, kv_heads, head_dim)
    value_rows = value[0].reshape(tok_rows, kv_heads, head_dim)
    gathered_queries, gathered_keys, gathered_values = (
        lax.all_to_all(queries, "ctx", split_axis=1, concat_axis=0, tiled=True),
        lax.all_to_all(key_rows, "ctx", split_axis=1, concat_axis=0, tiled=True),
        lax.all_to_all(value_rows, "ctx", split_axis=1, concat_axis=0, tiled=True),
    )
    mixed = lax.all_to_all(
        attend_whole(gathered_queries, gathered_keys, gathered_values, group),
        "ctx",
        split_axis=0,
        concat_axis=1,
        tiled=True,
    )
    layer_input = mixed.reshape(tok_rows, feature_width)
    filter_taps, filter_bias, input_weight, step_weight, step_bias, decay_log, skip_gain = (
        lax.all_gather(conv_weight, "dp", axis=1, tiled=True),
        lax.all_gather(conv_bias, "dp", axis=0, tiled=True),
        lax.all_gather(x_proj, "dp", axis=0, tiled=True),
        lax.all_gather(dt_proj, "dp", axis=1, tiled=True),
        lax.all_gather(dt_bias, "dp", axis=0, tiled=True),
        lax.all_gather(a_log, "dp", axis=1, tiled=True),
        lax.all_gather(d_skip, "dp", axis=0, tiled=True),
    )
    taps = filter_taps.shape[0]
    earlier = shifted(layer_input[tok_rows - (taps - 1) :], "ctx", 1)
    padded = jnp.concatenate([earlier, layer_input], axis=0).astype(jnp.float32)
    filtered = filter_bias.astype(jnp.float32)[None, :]
    for tap in range(taps):
        filtered = (
            filtered + filter_taps[tap].astype(jnp.float32)[None, :] * padded[tap : tap + tok_rows]
        )
    smoothed = jax.nn.silu(filtered).astype(jnp.bfloat16)
    projected = jnp.dot(smoothed, input_weight, preferred_element_type=jnp.float32)
    rank = step_weight.shape[0]
    states = decay_log.shape[0]
    low_rank = projected[:, :rank]
    normed = (
        low_rank * lax.rsqrt(jnp.mean(low_rank * low_rank, axis=-1, keepdims=True) + 1e-06)
    ).astype(jnp.bfloat16)
    step_size = jax.nn.softplus(
        jnp.dot(normed, step_weight, preferred_element_type=jnp.float32)
        + step_bias.astype(jnp.float32)[None, :]
    )
    input_gain = projected[:, rank : rank + states]
    readout = projected[:, rank + states : rank + 2 * states]
    decay_rate = -jnp.exp(decay_log.astype(jnp.float32))
    smooth_float = smoothed.astype(jnp.float32)
    drive_term = step_size * smooth_float
    empty_state = jnp.zeros((states, feature_width), jnp.float32)
    end_state, local_out = chain_pass(
        empty_state, step_size, drive_term, input_gain, readout, decay_rate
    )
    total_decay = jnp.exp(decay_rate * jnp.sum(step_size, axis=0)[None, :])

    def combine(earlier_pair, later_pair):
        return (earlier_pair[0] * later_pair[0], later_pair[0] * earlier_pair[1] + later_pair[1])

    _, carried = entering(
        (total_decay, end_state),
        "ctx",
        combine,
        (jnp.ones_like(total_decay), jnp.zeros_like(end_state)),
    )
    carried_out = carried_part(carried, step_size, readout, decay_rate)
    scan_out = local_out + carried_out + skip_gain.astype(jnp.float32)[None, :] * smooth_float
    gated = (scan_out * jax.nn.silu(gate_input[0].astype(jnp.float32))).astype(jnp.bfloat16)
    piece = lax.all_gather(out_proj, "dp", axis=0, tiled=True)
    columns = lax.slice_in_dim(gated, 0, piece.shape[0], axis=1)
    result = jnp.zeros((tok_rows, out_proj.shape[1]), jnp.float32) + jnp.dot(
        columns, piece, preferred_element_type=jnp.float32
    )
    return result.astype(jnp.bfloat16)[None]


HEAD = HEAD_SIZE
RANK = 256
STATES = 16
TAPS = 4
EPS = 1e-06
LOG2E = 1.4426950408889634
GROUP = 4
MEMBERS = (1, 8)
SLOTS = (2, 4, 16)
COST = {"attention": 5, "project": 0, "combine": 0, "scan": 8, "output": 0}
WAITS = {"project": (), "add": (), "combine": (), "scan": ()}
XW, DT, AL, MISC, PACK_ROWS = 0, 288, 544, 560, 576


def swap(value, distance, count):
    return lax.ppermute(value, "dp", [(i, i ^ distance) for i in range(count)])


def local_call(kernel, out_shape, name, weight=0, scratch=(), waits=(), away=0):
    def call(*args):
        inside, anywhere = (pl.BlockSpec(memory_space=m) for m in (pltpu.VMEM, pl.ANY))
        return pl.pallas_call(
            kernel,
            out_shape=out_shape,
            in_specs=[anywhere] * away + [inside] * (len(args) - away) + [anywhere] * len(waits),
            out_specs=jax.tree.map(lambda _: inside, out_shape),
            scratch_shapes=list(scratch),
            name=name,
            cost_estimate=pl.CostEstimate(flops=1, bytes_accessed=weight * 3_690_000, transcendentals=0),
            compiler_params=pltpu.CompilerParams(vmem_limit_bytes=48 * 1024 * 1024),
        )(*args, *waits)

    return call


def placed(distance):
    member = sum(1 << k for k, bit in enumerate(MEMBERS) if distance & bit)
    return member, sum(1 << k for k, bit in enumerate(SLOTS) if distance & bit)


def after(value, *others):
    return lax.optimization_barrier((value,) + others)[0]


def attention_kernel(*refs):
    inputs, (own_ref, across_ref, send_ref) = refs[:3], refs[3:6]
    q_ref, k_ref, v_ref, arrived = refs[6:]
    copies = [
        pltpu.make_async_copy(source, held, arrived.at[n])
        for n, (source, held) in enumerate(zip(inputs, (q_ref, k_ref, v_ref)))
    ]
    for copy in copies:
        copy.start()
    position = lax.axis_index("dp")
    rows = q_ref.shape[0]
    scale = 1.0 / math.sqrt(HEAD)
    row = lax.broadcasted_iota(jnp.int32, (GROUP, rows, rows), 1).reshape(GROUP * rows, rows)
    col = lax.broadcasted_iota(jnp.int32, (GROUP * rows, rows), 1)
    visible = col <= row
    for copy in copies:
        copy.wait()

    def lanes(index):
        return pl.ds(pl.multiple_of(index * HEAD, HEAD), HEAD)

    for pair in range(8):
        kv = (position // 4) ^ pair
        heads = [position ^ (pair * 4 + inner) for inner in range(4)]
        stacked = jnp.concatenate([q_ref[:, lanes(h)] for h in heads], axis=0)
        keys = k_ref[:, lanes(kv)]
        values = v_ref[:, lanes(kv)]
        scores = lax.dot_general(
            stacked, keys, (((1,), (1,)), ((), ())), preferred_element_type=jnp.float32
        )
        scores = jnp.where(visible, scores * scale, -jnp.inf)
        top = jnp.max(scores, axis=-1, keepdims=True)
        raised = jnp.exp(scores - top)
        total = jnp.sum(raised, axis=-1, keepdims=True)
        mixed = jnp.dot(raised.astype(jnp.bfloat16), values, preferred_element_type=jnp.float32)
        mixed = (mixed / total).astype(jnp.bfloat16)
        for inner in range(4):
            j, slot = placed(pair * 4 + inner)
            here = slice(slot * HEAD, (slot + 1) * HEAD)
            target = (own_ref, send_ref.at[0], across_ref, send_ref.at[1])[j]
            target[:, here] = mixed[inner * rows : (inner + 1) * rows]


def gates_kernel(g_ref, own_ref, across_ref, send_ref):
    position = lax.axis_index("dp")
    for distance in range(32):
        j, slot = placed(distance)
        here = slice(slot * HEAD, (slot + 1) * HEAD)
        head = position ^ distance
        target = (own_ref, send_ref.at[0], across_ref, send_ref.at[1])[j]
        target[:, here] = g_ref[:, pl.ds(pl.multiple_of(head * HEAD, HEAD), HEAD)]


def slot_packs(refs):
    own, z_ref, x_ref, y_ref, xy_ref, xyz_ref = refs
    return [
        own,
        x_ref.at[:PACK_ROWS],
        y_ref.at[:PACK_ROWS],
        xy_ref,
        z_ref,
        x_ref.at[PACK_ROWS:],
        y_ref.at[PACK_ROWS:],
        xyz_ref,
    ]


def project_kernel(*refs):
    packs = slot_packs(refs[:6])
    own_ref, send_ref, pair_ref = refs[6:9]
    smooth_ref, pkeep_ref, psend_ref, weight_ref = refs[-4:]
    sources = [own_ref, send_ref.at[0], pair_ref.at[0], pair_ref.at[1]]
    rows = own_ref.shape[0]
    row = lax.broadcasted_iota(jnp.int32, (rows, HEAD), 0)
    masks = [row >= k for k in range(TAPS)]
    for slot in range(8):
        here = slice(slot * HEAD, (slot + 1) * HEAD)
        weight_ref[:, here] = packs[slot][XW : XW + 288, :]
        misc = packs[slot][MISC : MISC + 16, :].astype(jnp.float32)
        for j in range(GROUP):
            mixed = sources[j][:, here].astype(jnp.float32)
            filtered = misc[4:5] + jnp.zeros_like(mixed)
            for tap in range(TAPS):
                shift = TAPS - 1 - tap
                moved = mixed
                if shift:
                    moved = jnp.where(masks[shift], pltpu.roll(mixed, shift, 0), 0.0)
                filtered = filtered + misc[tap : tap + 1] * moved
            smooth = filtered / (1.0 + jnp.exp(-filtered))
            smooth_ref[j, :, here] = smooth.astype(jnp.bfloat16)
    for j in range(GROUP):
        part = lax.dot_general(
            smooth_ref[j],
            weight_ref[...],
            (((1,), (1,)), ((), ())),
            preferred_element_type=jnp.float32,
        )
        target = psend_ref if j % 2 else pkeep_ref
        half = j // 2
        target[:, half * 256 : half * 256 + 256] = part[:, :256]
        target[:, 512 + half * 32 : 512 + half * 32 + 32] = part[:, 256:288]


def add_kernel(a_ref, b_ref, *rest):
    rest[-1][...] = a_ref[...] + b_ref[...]


def combine_kernel(chip_ref, other_ref, *rest):
    full_ref = rest[-1]
    full_ref[:, :256] = chip_ref[:, :256] + other_ref[:, 256:512]
    full_ref[:, 256:512] = chip_ref[:, 256:512] + other_ref[:, :256]
    lanes = lax.broadcasted_iota(jnp.int32, (chip_ref.shape[0], HEAD), 1)
    other = other_ref[:, 512:]
    turned = jnp.where(lanes < 32, pltpu.roll(other, HEAD - 32, 1), pltpu.roll(other, 32, 1))
    full_ref[:, 512:] = chip_ref[:, 512:] + turned


def scan_kernel(half, *refs):
    packs, (f0_ref, f1_ref, smooth_ref) = slot_packs(refs[:6]), refs[6:9]
    scanned_ref, size_ref, drive_ref, out_ref, rate_ref, gain_ref, read_ref = refs[-7:]
    rows = f0_ref.shape[0]
    sources = [f0_ref, f1_ref]
    for s in range(2):
        low = sources[s][:, half * 256 : half * 256 + 256]
        normed = low * lax.rsqrt(jnp.mean(low * low, axis=-1, keepdims=True) + EPS)
        normed = normed.astype(jnp.bfloat16)
        both = sources[s][:, 512 + half * 32 : 512 + half * 32 + 32]
        for n in range(STATES):
            wide = jnp.broadcast_to(both[:, n : n + 1], (rows, HEAD))
            gain_ref[s, pl.ds(n, rows, stride=STATES), :] = wide
            wide = jnp.broadcast_to(both[:, STATES + n : STATES + n + 1], (rows, HEAD))
            read_ref[s, pl.ds(n, rows, stride=STATES), :] = wide
        for slot in range(8):
            bias = packs[slot][MISC : MISC + 16, :].astype(jnp.float32)[5:6]
            raw = (
                jnp.dot(
                    normed, packs[slot][DT : DT + RANK, :], preferred_element_type=jnp.float32
                )
                + bias
            )
            size = jnp.maximum(raw, 0.0) + jnp.log1p(jnp.exp(-jnp.abs(raw)))
            smooth = smooth_ref[2 * half + s, :, slot * HEAD : (slot + 1) * HEAD]
            size_ref[s, pl.ds(slot, rows, stride=8), :] = size
            drive_ref[s, pl.ds(slot, rows, stride=8), :] = size * smooth.astype(jnp.float32)
    for slot in range(8):
        rate = -jnp.exp(packs[slot][AL : AL + STATES, :].astype(jnp.float32)) * LOG2E
        rate_ref[pl.ds(slot, STATES, stride=8), :] = rate

    def one(t, states):
        new = []
        for s in range(2):
            at = pl.ds(pl.multiple_of(t * 8, 8), 8)
            size = size_ref[s, at, :]
            drive = drive_ref[s, at, :]
            total = [None, None]
            for n in range(STATES):
                decay = jnp.exp2(size * rate_ref[n * 8 : n * 8 + 8, :])
                gain = gain_ref[s, pl.ds(t * STATES + n, 1), :]
                read = read_ref[s, pl.ds(t * STATES + n, 1), :]
                state = decay * states[s * STATES + n] + gain * drive
                new.append(state)
                term = read * state
                total[n % 2] = term if total[n % 2] is None else total[n % 2] + term
            out_ref[s, at, :] = total[0] + total[1]
        return tuple(new)

    zero = jnp.zeros((8, HEAD), jnp.float32)
    lax.fori_loop(0, rows, one, (zero,) * (2 * STATES), unroll=2)
    for s in range(2):
        for slot in range(8):
            here = slice(slot * HEAD, (slot + 1) * HEAD)
            skip = packs[slot][MISC : MISC + 16, :].astype(jnp.float32)[6:7]
            smooth = smooth_ref[2 * half + s, :, here].astype(jnp.float32)
            scanned = out_ref[s, pl.ds(slot, rows, stride=8), :] + skip * smooth
            scanned_ref[s, :, here] = scanned


def output_kernel(half, *refs):
    slots = refs[:-6]
    scanned_ref, g0_ref, g1_ref, keep_ref, send_ref, gated_ref = refs[-6:]
    rows = keep_ref.shape[0]
    gates = [g0_ref.at[0] if half else g0_ref, g1_ref.at[half]]
    for s in range(2):
        for slot in range(8):
            here = slice(slot * HEAD, (slot + 1) * HEAD)
            gate = gates[s][:, here].astype(jnp.float32)
            gated = scanned_ref[s, :, here] * (gate / (1.0 + jnp.exp(-gate)))
            gated_ref[s * rows : (s + 1) * rows, here] = gated.astype(jnp.bfloat16)
    width = 512
    for begin in range(0, keep_ref.shape[1], width):
        columns = slice(begin, begin + width)
        weight = jnp.concatenate([slot[:, columns] for slot in slots], axis=0)
        total = jnp.dot(gated_ref[...], weight, preferred_element_type=jnp.float32)
        keep_ref[:, columns] = total[:rows]
        send_ref[:, columns] = total[rows:].astype(send_ref.dtype)


def grouped(query, key, value, gate_input, conv_weight, conv_bias, x_proj, dt_proj, dt_bias, a_log, d_skip, out_proj):
    count = lax.axis_size("dp")
    rows = query.shape[1]
    width = out_proj.shape[1]
    pack = jnp.concatenate(
        [
            x_proj.T,
            dt_proj,
            a_log,
            conv_weight,
            conv_bias[None],
            dt_bias[None],
            d_skip[None],
            jnp.zeros((PACK_ROWS - MISC - 7, HEAD), jnp.bfloat16),
        ],
        axis=0,
    )

    near, far = MEMBERS
    bit_x, bit_y, bit_z = SLOTS

    pack_z = swap(pack, bit_z, count)
    slot_x = swap(out_proj, bit_x, count)
    slot_y = swap(out_proj, bit_y, count)
    pack_two = jnp.concatenate([pack, pack_z], axis=0)
    pack_x = swap(pack_two, bit_x, count)
    pack_y = swap(pack_two, bit_y, count)
    pack_xy = swap(after(pack_y[:PACK_ROWS], slot_x), bit_x, count)
    pack_xyz = swap(after(pack_x[PACK_ROWS:], slot_y), bit_y, count)
    packs = [pack, pack_z, pack_x, pack_y, pack_xy, pack_xyz]
    slot_xy = swap(slot_y, bit_x, count)
    slot_z = swap(out_proj, bit_z, count)
    slot_zx = swap(slot_z, bit_x, count)
    slot_zy = swap(slot_z, bit_y, count)
    slot_zxy = swap(slot_zx, bit_y, count)
    slots = [out_proj, slot_x, slot_y, slot_xy, slot_z, slot_zx, slot_zy, slot_zxy]

    quarter = jax.ShapeDtypeStruct((rows, 8 * HEAD), jnp.bfloat16)
    both = jax.ShapeDtypeStruct((2, rows, 8 * HEAD), jnp.bfloat16)

    def spread(own, across, send):
        arrived = swap(send, near, count)
        pair = swap(jnp.stack([across, arrived[1]]), far, count)
        return own, arrived, pair

    made = local_call(
        attention_kernel,
        (quarter, quarter, both),
        "attention",
        COST["attention"],
        scratch=[
            pltpu.VMEM(query.shape[1:], jnp.bfloat16),
            pltpu.VMEM(key.shape[1:], jnp.bfloat16),
            pltpu.VMEM(value.shape[1:], jnp.bfloat16),
            pltpu.SemaphoreType.DMA((3,)),
        ],
        away=3,
    )(query[0], key[0], value[0])
    mixed = spread(*made)
    wide = jax.ShapeDtypeStruct((rows, 640), jnp.float32)
    smooth, pkeep, psend = local_call(
        project_kernel,
        (jax.ShapeDtypeStruct((GROUP, rows, 8 * HEAD), jnp.bfloat16), wide, wide),
        "project",
        COST["project"],
        scratch=[pltpu.VMEM((288, 8 * HEAD), jnp.bfloat16)],
        waits=[slots[i] for i in WAITS["project"]],
    )(*packs, *mixed)
    chip = local_call(
        add_kernel, wide, "add", waits=[slots[i] for i in WAITS["add"]]
    )(pkeep, swap(psend, near, count))
    full = local_call(
        combine_kernel, wide, "combine", COST["combine"], waits=[slots[i] for i in WAITS["combine"]]
    )(chip, swap(chip, far, count))
    partner = swap(full, near, count)
    gate_source = after(gate_input[0], psend)
    gates = spread(*local_call(gates_kernel, (quarter, quarter, both), "gates")(gate_source))

    def scanned(which, waits):
        work = pltpu.VMEM((2, rows * 8, HEAD), jnp.float32)
        lanes = pltpu.VMEM((2, rows * STATES, HEAD), jnp.float32)
        return local_call(
            functools.partial(scan_kernel, which),
            jax.ShapeDtypeStruct((2, rows, 8 * HEAD), jnp.float32),
            "scan",
            COST["scan"],
            scratch=[work, work, work, pltpu.VMEM((STATES * 8, HEAD), jnp.float32), lanes, lanes],
            waits=waits,
        )(*packs, full, partner, smooth)

    def projected_out(which, *args):
        return local_call(
            functools.partial(output_kernel, which),
            (
                jax.ShapeDtypeStruct((rows, width), jnp.float32),
                jax.ShapeDtypeStruct((rows, width), jnp.bfloat16),
            ),
            "output",
            COST["output"],
            scratch=[pltpu.VMEM((2 * rows, 8 * HEAD), jnp.bfloat16)],
        )(*slots, *args)

    own_gate, sent_gate, pair_gate = gates
    far_keep, far_send = projected_out(
        1, scanned(1, [slots[i] for i in WAITS["scan"]]), pair_gate, pair_gate
    )
    far_sum = (far_keep + swap(far_send, near, count).astype(jnp.float32)).astype(jnp.bfloat16)
    from_far = swap(far_sum, far, count)
    near_keep, near_send = projected_out(0, scanned(0, [far_sum]), own_gate, sent_gate)
    from_near = swap(after(near_send, from_far), near, count)
    near_sum = near_keep + from_near.astype(jnp.float32) + from_far.astype(jnp.float32)
    return near_sum.astype(jnp.bfloat16)[None]


def solution(mesh):
    placed = (
        P("dp", "ctx", None),
        P("dp", "ctx", None),
        P("dp", "ctx", None),
        P("dp", "ctx", None),
        P(None, "dp"),
        P("dp"),
        P("dp", None),
        P(None, "dp"),
        P("dp"),
        P(None, "dp"),
        P("dp"),
        P("dp", None),
    )
    fits = mesh.shape["ctx"] == 1 and mesh.shape["dp"] == 32
    return jax.shard_map(
        grouped if fits else shards, mesh=mesh, in_specs=placed, out_specs=P("dp", "ctx", None), check_vma=False
    )
```

```python
import functools
import math

import jax
import jax.numpy as jnp
from jax import lax
from jax.experimental import pallas as pl
from jax.experimental.pallas import tpu as pltpu
from jax.sharding import PartitionSpec as P

HEAD_SIZE = 128


def shifted(value, axis, steps):
    count = lax.axis_size(axis)
    initial, last = (max(0, -steps), min(count, count - steps))
    return lax.ppermute(value, axis, [(source, source + steps) for source in range(initial, last)])


def entering(shard, axis, combine, identity):
    size, position = (lax.axis_size(axis), lax.axis_index(axis))
    everything = jax.tree.map(lambda part: lax.all_gather(part, axis), shard)
    start = jax.tree.map(
        lambda part, zero: jnp.broadcast_to(jnp.asarray(zero, part.dtype), part.shape),
        shard,
        identity,
    )

    def hop(k, before):
        reached = k < position
        new = combine(before, jax.tree.map(lambda part: part[k], everything))
        return jax.tree.map(lambda a, b: jnp.where(reached, a, b), new, before)

    return lax.fori_loop(0, size, hop, start)


def attend_whole(queries, keys_all, values_all, group):
    seq_len, kv_local, head_dim = keys_all.shape
    scale = 1.0 / math.sqrt(head_dim)
    block = min(512, seq_len)
    pieces = []
    for index in range(seq_len // block):
        begin = index * block
        end = begin + block
        query_block = queries[begin:end].reshape(block, kv_local, group, head_dim)
        scores = (
            jnp.einsum(
                "rgqd,ngd->gqrn", query_block, keys_all[:end], preferred_element_type=jnp.float32
            )
            * scale
        )
        visible = jnp.arange(end)[None, :] <= (begin + jnp.arange(block))[:, None]
        scores = jnp.where(visible, scores, -jnp.inf)
        top = jnp.max(scores, axis=-1, keepdims=True)
        raised = jnp.exp(scores - top)
        total = jnp.sum(raised, axis=-1)
        mixed = jnp.einsum(
            "gqrn,ngd->rgqd",
            raised.astype(jnp.bfloat16),
            values_all[:end],
            preferred_element_type=jnp.float32,
        )
        mixed = mixed / jnp.transpose(total, (2, 0, 1))[..., None]
        pieces.append(mixed.astype(jnp.bfloat16).reshape(block, kv_local, group * head_dim))
    return jnp.concatenate(pieces, axis=0)


def chain_pass(initial, step_size, drive_term, input_gain, readout, decay_rate):
    tok_rows = step_size.shape[0]
    block_len = math.gcd(tok_rows, 32)
    blocks = tok_rows // block_len

    def advance(state, inputs):
        size_block, drive_block, gain_block, read_block = inputs
        outputs = []
        for position in range(block_len):
            state = jnp.exp(size_block[position][None, :] * decay_rate) * state
            state = state + gain_block[position][:, None] * drive_block[position][None, :]
            outputs.append(jnp.dot(read_block[position], state, precision=lax.Precision.HIGHEST))
        return (state, jnp.stack(outputs))

    inputs = tuple(
        (
            item.reshape((blocks, block_len) + item.shape[1:])
            for item in (step_size, drive_term, input_gain, readout)
        )
    )
    final, outputs = lax.scan(advance, initial, inputs)
    return (final, outputs.reshape(tok_rows, -1))


def carried_part(carried, step_size, readout, decay_rate):
    tok_rows, channels = step_size.shape
    lower = (jnp.arange(tok_rows)[:, None] >= jnp.arange(tok_rows)[None, :]).astype(jnp.float32)
    cumulative = jnp.dot(lower, step_size, precision=lax.Precision.HIGHEST)
    block_len = math.gcd(tok_rows, 32)
    blocks = tok_rows // block_len
    cum_blocks = cumulative.reshape(blocks, block_len, channels)
    read_blocks = readout.reshape(blocks, block_len, readout.shape[1])

    def one_block(items):
        cum_block, read_block = items
        factor = jnp.exp(cum_block[:, None, :] * decay_rate[None])
        return jnp.sum(read_block[:, :, None] * factor * carried[None], axis=1)

    return lax.map(one_block, (cum_blocks, read_blocks)).reshape(tok_rows, channels)


def shards(
    query,
    key,
    value,
    gate_input,
    conv_weight,
    conv_bias,
    x_proj,
    dt_proj,
    dt_bias,
    a_log,
    d_skip,
    out_proj,
):
    tok_rows = query.shape[1]
    feature_width = query.shape[2]
    head_dim = HEAD_SIZE
    kv_heads = key.shape[2] // head_dim
    group = feature_width // key.shape[2]
    queries = query[0].reshape(tok_rows, kv_heads, group * head_dim)
    key_rows = key[0].reshape(tok_rows, kv_heads, head_dim)
    value_rows = value[0].reshape(tok_rows, kv_heads, head_dim)
    gathered_queries, gathered_keys, gathered_values = (
        lax.all_to_all(queries, "ctx", split_axis=1, concat_axis=0, tiled=True),
        lax.all_to_all(key_rows, "ctx", split_axis=1, concat_axis=0, tiled=True),
        lax.all_to_all(value_rows, "ctx", split_axis=1, concat_axis=0, tiled=True),
    )
    mixed = lax.all_to_all(
        attend_whole(gathered_queries, gathered_keys, gathered_values, group),
        "ctx",
        split_axis=0,
        concat_axis=1,
        tiled=True,
    )
    layer_input = mixed.reshape(tok_rows, feature_width)
    filter_taps, filter_bias, input_weight, step_weight, step_bias, decay_log, skip_gain = (
        lax.all_gather(conv_weight, "dp", axis=1, tiled=True),
        lax.all_gather(conv_bias, "dp", axis=0, tiled=True),
        lax.all_gather(x_proj, "dp", axis=0, tiled=True),
        lax.all_gather(dt_proj, "dp", axis=1, tiled=True),
        lax.all_gather(dt_bias, "dp", axis=0, tiled=True),
        lax.all_gather(a_log, "dp", axis=1, tiled=True),
        lax.all_gather(d_skip, "dp", axis=0, tiled=True),
    )
    taps = filter_taps.shape[0]
    earlier = shifted(layer_input[tok_rows - (taps - 1) :], "ctx", 1)
    padded = jnp.concatenate([earlier, layer_input], axis=0).astype(jnp.float32)
    filtered = filter_bias.astype(jnp.float32)[None, :]
    for tap in range(taps):
        filtered = (
            filtered + filter_taps[tap].astype(jnp.float32)[None, :] * padded[tap : tap + tok_rows]
        )
    smoothed = jax.nn.silu(filtered).astype(jnp.bfloat16)
    projected = jnp.dot(smoothed, input_weight, preferred_element_type=jnp.float32)
    rank = step_weight.shape[0]
    states = decay_log.shape[0]
    low_rank = projected[:, :rank]
    normed = (
        low_rank * lax.rsqrt(jnp.mean(low_rank * low_rank, axis=-1, keepdims=True) + 1e-06)
    ).astype(jnp.bfloat16)
    step_size = jax.nn.softplus(
        jnp.dot(normed, step_weight, preferred_element_type=jnp.float32)
        + step_bias.astype(jnp.float32)[None, :]
    )
    input_gain = projected[:, rank : rank + states]
    readout = projected[:, rank + states : rank + 2 * states]
    decay_rate = -jnp.exp(decay_log.astype(jnp.float32))
    smooth_float = smoothed.astype(jnp.float32)
    drive_term = step_size * smooth_float
    empty_state = jnp.zeros((states, feature_width), jnp.float32)
    end_state, local_out = chain_pass(
        empty_state, step_size, drive_term, input_gain, readout, decay_rate
    )
    total_decay = jnp.exp(decay_rate * jnp.sum(step_size, axis=0)[None, :])

    def combine(earlier_pair, later_pair):
        return (earlier_pair[0] * later_pair[0], later_pair[0] * earlier_pair[1] + later_pair[1])

    _, carried = entering(
        (total_decay, end_state),
        "ctx",
        combine,
        (jnp.ones_like(total_decay), jnp.zeros_like(end_state)),
    )
    carried_out = carried_part(carried, step_size, readout, decay_rate)
    scan_out = local_out + carried_out + skip_gain.astype(jnp.float32)[None, :] * smooth_float
    gated = (scan_out * jax.nn.silu(gate_input[0].astype(jnp.float32))).astype(jnp.bfloat16)
    piece = lax.all_gather(out_proj, "dp", axis=0, tiled=True)
    columns = lax.slice_in_dim(gated, 0, piece.shape[0], axis=1)
    result = jnp.zeros((tok_rows, out_proj.shape[1]), jnp.float32) + jnp.dot(
        columns, piece, preferred_element_type=jnp.float32
    )
    return result.astype(jnp.bfloat16)[None]


HEAD = HEAD_SIZE
RANK = 256
STATES = 16
TAPS = 4
EPS = 1e-06
LOG2E = 1.4426950408889634
GROUP = 4
MEMBERS = (1, 8)
SLOTS = (2, 4, 16)
COST = {"attention": 5, "project": 0, "combine": 0, "scan": 8, "output": 0}
WAITS = {"project": (4,), "add": (), "combine": (), "scan": ()}
XW, DT, AL, MISC, PACK_ROWS = 0, 288, 544, 560, 576


def swap(value, distance, count):
    return lax.ppermute(value, "dp", [(i, i ^ distance) for i in range(count)])


def local_call(kernel, out_shape, name, weight=0, scratch=(), waits=(), away=0):
    def call(*args):
        inside, anywhere = (pl.BlockSpec(memory_space=m) for m in (pltpu.VMEM, pl.ANY))
        return pl.pallas_call(
            kernel,
            out_shape=out_shape,
            in_specs=[anywhere] * away + [inside] * (len(args) - away) + [anywhere] * len(waits),
            out_specs=jax.tree.map(lambda _: inside, out_shape),
            scratch_shapes=list(scratch),
            name=name,
            cost_estimate=pl.CostEstimate(flops=1, bytes_accessed=weight * 3_690_000, transcendentals=0),
            compiler_params=pltpu.CompilerParams(vmem_limit_bytes=20 * 1024 * 1024),
        )(*args, *waits)

    return call


def placed(distance):
    member = sum(1 << k for k, bit in enumerate(MEMBERS) if distance & bit)
    return member, sum(1 << k for k, bit in enumerate(SLOTS) if distance & bit)


def after(value, *others):
    return lax.optimization_barrier((value,) + others)[0]


def attention_kernel(*refs):
    inputs, (own_ref, across_ref, send_ref) = refs[:3], refs[3:6]
    q_ref, k_ref, v_ref, arrived = refs[6:]
    copies = [
        pltpu.make_async_copy(source, held, arrived.at[n])
        for n, (source, held) in enumerate(zip(inputs, (q_ref, k_ref, v_ref)))
    ]
    for copy in copies:
        copy.start()
    position = lax.axis_index("dp")
    rows = q_ref.shape[0]
    scale = 1.0 / math.sqrt(HEAD)
    row = lax.broadcasted_iota(jnp.int32, (GROUP, rows, rows), 1).reshape(GROUP * rows, rows)
    col = lax.broadcasted_iota(jnp.int32, (GROUP * rows, rows), 1)
    visible = col <= row
    for copy in copies:
        copy.wait()

    def lanes(index):
        return pl.ds(pl.multiple_of(index * HEAD, HEAD), HEAD)

    for pair in range(8):
        kv = (position // 4) ^ pair
        heads = [position ^ (pair * 4 + inner) for inner in range(4)]
        stacked = jnp.concatenate([q_ref[:, lanes(h)] for h in heads], axis=0)
        keys = k_ref[:, lanes(kv)]
        values = v_ref[:, lanes(kv)]
        scores = lax.dot_general(
            stacked, keys, (((1,), (1,)), ((), ())), preferred_element_type=jnp.float32
        )
        scores = jnp.where(visible, scores * scale, -jnp.inf)
        top = jnp.max(scores, axis=-1, keepdims=True)
        raised = jnp.exp(scores - top)
        total = jnp.sum(raised, axis=-1, keepdims=True)
        mixed = jnp.dot(raised.astype(jnp.bfloat16), values, preferred_element_type=jnp.float32)
        mixed = (mixed / total).astype(jnp.bfloat16)
        for inner in range(4):
            j, slot = placed(pair * 4 + inner)
            here = slice(slot * HEAD, (slot + 1) * HEAD)
            target = (own_ref, send_ref.at[0], across_ref, send_ref.at[1])[j]
            target[:, here] = mixed[inner * rows : (inner + 1) * rows]


def gates_kernel(g_ref, own_ref, across_ref, send_ref):
    position = lax.axis_index("dp")
    for distance in range(32):
        j, slot = placed(distance)
        here = slice(slot * HEAD, (slot + 1) * HEAD)
        head = position ^ distance
        target = (own_ref, send_ref.at[0], across_ref, send_ref.at[1])[j]
        target[:, here] = g_ref[:, pl.ds(pl.multiple_of(head * HEAD, HEAD), HEAD)]


def slot_packs(refs):
    own, z_ref, x_ref, y_ref, xy_ref, xyz_ref = refs
    return [
        own,
        x_ref.at[:PACK_ROWS],
        y_ref.at[:PACK_ROWS],
        xy_ref,
        z_ref,
        x_ref.at[PACK_ROWS:],
        y_ref.at[PACK_ROWS:],
        xyz_ref,
    ]


def project_kernel(*refs):
    packs = slot_packs(refs[:6])
    own_ref, send_ref, pair_ref = refs[6:9]
    smooth_ref, pkeep_ref, psend_ref, weight_ref = refs[-4:]
    sources = [own_ref, send_ref.at[0], pair_ref.at[0], pair_ref.at[1]]
    rows = own_ref.shape[0]
    row = lax.broadcasted_iota(jnp.int32, (rows, HEAD), 0)
    masks = [row >= k for k in range(TAPS)]
    for slot in range(8):
        here = slice(slot * HEAD, (slot + 1) * HEAD)
        weight_ref[:, here] = packs[slot][XW : XW + 288, :]
        misc = packs[slot][MISC : MISC + 16, :].astype(jnp.float32)
        for j in range(GROUP):
            mixed = sources[j][:, here].astype(jnp.float32)
            filtered = misc[4:5] + jnp.zeros_like(mixed)
            for tap in range(TAPS):
                shift = TAPS - 1 - tap
                moved = mixed
                if shift:
                    moved = jnp.where(masks[shift], pltpu.roll(mixed, shift, 0), 0.0)
                filtered = filtered + misc[tap : tap + 1] * moved
            smooth = filtered / (1.0 + jnp.exp(-filtered))
            smooth_ref[j, :, here] = smooth.astype(jnp.bfloat16)
    for j in range(GROUP):
        part = lax.dot_general(
            smooth_ref[j],
            weight_ref[...],
            (((1,), (1,)), ((), ())),
            preferred_element_type=jnp.float32,
        )
        target = psend_ref if j % 2 else pkeep_ref
        half = j // 2
        target[:, half * 256 : half * 256 + 256] = part[:, :256]
        target[:, 512 + half * 32 : 512 + half * 32 + 32] = part[:, 256:288]


def join_kernel(a_ref, b_ref, *rest):
    out_ref = rest[-1]
    out_ref[:PACK_ROWS] = a_ref[...]
    out_ref[PACK_ROWS:] = b_ref[...]


def add_kernel(a_ref, b_ref, *rest):
    rest[-1][...] = a_ref[...] + b_ref[...]


def combine_kernel(chip_ref, other_ref, *rest):
    full_ref = rest[-1]
    full_ref[:, :256] = chip_ref[:, :256] + other_ref[:, 256:512]
    full_ref[:, 256:512] = chip_ref[:, 256:512] + other_ref[:, :256]
    lanes = lax.broadcasted_iota(jnp.int32, (chip_ref.shape[0], HEAD), 1)
    other = other_ref[:, 512:]
    turned = jnp.where(lanes < 32, pltpu.roll(other, HEAD - 32, 1), pltpu.roll(other, 32, 1))
    full_ref[:, 512:] = chip_ref[:, 512:] + turned


def scan_kernel(half, *refs):
    packs, (f0_ref, f1_ref, smooth_ref) = slot_packs(refs[:6]), refs[6:9]
    scanned_ref, size_ref, drive_ref, out_ref, rate_ref, gain_ref, read_ref = refs[-7:]
    rows = f0_ref.shape[0]
    sources = [f0_ref, f1_ref]
    for s in range(2):
        low = sources[s][:, half * 256 : half * 256 + 256]
        normed = low * lax.rsqrt(jnp.mean(low * low, axis=-1, keepdims=True) + EPS)
        normed = normed.astype(jnp.bfloat16)
        both = sources[s][:, 512 + half * 32 : 512 + half * 32 + 32]
        for n in range(STATES):
            wide = jnp.broadcast_to(both[:, n : n + 1], (rows, HEAD))
            gain_ref[s, pl.ds(n, rows, stride=STATES), :] = wide
            wide = jnp.broadcast_to(both[:, STATES + n : STATES + n + 1], (rows, HEAD))
            read_ref[s, pl.ds(n, rows, stride=STATES), :] = wide
        for slot in range(8):
            bias = packs[slot][MISC : MISC + 16, :].astype(jnp.float32)[5:6]
            raw = (
                jnp.dot(
                    normed, packs[slot][DT : DT + RANK, :], preferred_element_type=jnp.float32
                )
                + bias
            )
            size = jnp.maximum(raw, 0.0) + jnp.log1p(jnp.exp(-jnp.abs(raw)))
            smooth = smooth_ref[2 * half + s, :, slot * HEAD : (slot + 1) * HEAD]
            size_ref[s, pl.ds(slot, rows, stride=8), :] = size
            drive_ref[s, pl.ds(slot, rows, stride=8), :] = size * smooth.astype(jnp.float32)
    for slot in range(8):
        rate = -jnp.exp(packs[slot][AL : AL + STATES, :].astype(jnp.float32)) * LOG2E
        rate_ref[pl.ds(slot, STATES, stride=8), :] = rate

    def one(t, states):
        new = []
        for s in range(2):
            at = pl.ds(pl.multiple_of(t * 8, 8), 8)
            size = size_ref[s, at, :]
            drive = drive_ref[s, at, :]
            total = [None, None]
            for n in range(STATES):
                decay = jnp.exp2(size * rate_ref[n * 8 : n * 8 + 8, :])
                gain = gain_ref[s, pl.ds(t * STATES + n, 1), :]
                read = read_ref[s, pl.ds(t * STATES + n, 1), :]
                state = decay * states[s * STATES + n] + gain * drive
                new.append(state)
                term = read * state
                total[n % 2] = term if total[n % 2] is None else total[n % 2] + term
            out_ref[s, at, :] = total[0] + total[1]
        return tuple(new)

    zero = jnp.zeros((8, HEAD), jnp.float32)
    lax.fori_loop(0, rows, one, (zero,) * (2 * STATES), unroll=2)
    for s in range(2):
        for slot in range(8):
            here = slice(slot * HEAD, (slot + 1) * HEAD)
            skip = packs[slot][MISC : MISC + 16, :].astype(jnp.float32)[6:7]
            smooth = smooth_ref[2 * half + s, :, here].astype(jnp.float32)
            scanned = out_ref[s, pl.ds(slot, rows, stride=8), :] + skip * smooth
            scanned_ref[s, :, here] = scanned


def output_kernel(half, *refs):
    slots = refs[:-6]
    scanned_ref, g0_ref, g1_ref, keep_ref, send_ref, gated_ref = refs[-6:]
    rows = keep_ref.shape[0]
    gates = [g0_ref.at[0] if half else g0_ref, g1_ref.at[half]]
    for s in range(2):
        for slot in range(8):
            here = slice(slot * HEAD, (slot + 1) * HEAD)
            gate = gates[s][:, here].astype(jnp.float32)
            gated = scanned_ref[s, :, here] * (gate / (1.0 + jnp.exp(-gate)))
            gated_ref[s * rows : (s + 1) * rows, here] = gated.astype(jnp.bfloat16)
    width = 512
    for begin in range(0, keep_ref.shape[1], width):
        columns = slice(begin, begin + width)
        weight = jnp.concatenate([slot[:, columns] for slot in slots], axis=0)
        total = jnp.dot(gated_ref[...], weight, preferred_element_type=jnp.float32)
        keep_ref[:, columns] = total[:rows]
        send_ref[:, columns] = total[rows:].astype(send_ref.dtype)


def grouped(query, key, value, gate_input, conv_weight, conv_bias, x_proj, dt_proj, dt_bias, a_log, d_skip, out_proj):
    count = lax.axis_size("dp")
    rows = query.shape[1]
    width = out_proj.shape[1]
    pack = jnp.concatenate(
        [
            x_proj.T,
            dt_proj,
            a_log,
            conv_weight,
            conv_bias[None],
            dt_bias[None],
            d_skip[None],
            jnp.zeros((PACK_ROWS - MISC - 7, HEAD), jnp.bfloat16),
        ],
        axis=0,
    )

    near, far = MEMBERS
    bit_x, bit_y, bit_z = SLOTS

    quarter = jax.ShapeDtypeStruct((rows, 8 * HEAD), jnp.bfloat16)
    both = jax.ShapeDtypeStruct((2, rows, 8 * HEAD), jnp.bfloat16)

    def spread(own, across, send):
        arrived = swap(send, near, count)
        pair = swap(jnp.stack([across, arrived[1]]), far, count)
        return own, arrived, pair

    made = local_call(
        attention_kernel,
        (quarter, quarter, both),
        "attention",
        COST["attention"],
        scratch=[
            pltpu.VMEM(query.shape[1:], jnp.bfloat16),
            pltpu.VMEM(key.shape[1:], jnp.bfloat16),
            pltpu.VMEM(value.shape[1:], jnp.bfloat16),
            pltpu.SemaphoreType.DMA((3,)),
        ],
        away=3,
    )(query[0], key[0], value[0])
    mixed = spread(*made)
    pack_z = swap(pack, bit_z, count)
    slot_x = swap(out_proj, bit_x, count)
    slot_y = swap(out_proj, bit_y, count)
    pack_two = local_call(join_kernel, jax.ShapeDtypeStruct((2 * PACK_ROWS, HEAD), jnp.bfloat16), "join", waits=[slot_x, slot_y])(pack, pack_z)
    pack_x = swap(pack_two, bit_x, count)
    pack_y = swap(pack_two, bit_y, count)
    pack_xy = swap(pack_y[:PACK_ROWS], bit_x, count)
    pack_xyz = swap(pack_x[PACK_ROWS:], bit_y, count)
    packs = [pack, pack_z, pack_x, pack_y, pack_xy, pack_xyz]
    slot_xy = swap(slot_y, bit_x, count)
    slot_z = swap(after(out_proj, mixed[1]), bit_z, count)
    slot_zx = swap(slot_z, bit_x, count)
    slot_zy = swap(slot_z, bit_y, count)
    slot_zxy = swap(slot_zx, bit_y, count)
    slots = [out_proj, slot_x, slot_y, slot_xy, slot_z, slot_zx, slot_zy, slot_zxy]

    wide = jax.ShapeDtypeStruct((rows, 640), jnp.float32)
    smooth, pkeep, psend = local_call(
        project_kernel,
        (jax.ShapeDtypeStruct((GROUP, rows, 8 * HEAD), jnp.bfloat16), wide, wide),
        "project",
        COST["project"],
        scratch=[pltpu.VMEM((288, 8 * HEAD), jnp.bfloat16)],
        waits=[slots[i] for i in WAITS["project"]],
    )(*packs, *mixed)
    chip = local_call(
        add_kernel, wide, "add", waits=[slots[i] for i in WAITS["add"]]
    )(pkeep, swap(psend, near, count))
    full = local_call(
        combine_kernel, wide, "combine", COST["combine"], waits=[slots[i] for i in WAITS["combine"]]
    )(chip, swap(chip, far, count))
    partner = swap(full, near, count)
    gate_source = after(gate_input[0], chip)
    gates = spread(*local_call(gates_kernel, (quarter, quarter, both), "gates")(gate_source))

    def scanned(which, waits):
        work = pltpu.VMEM((2, rows * 8, HEAD), jnp.float32)
        lanes = pltpu.VMEM((2, rows * STATES, HEAD), jnp.float32)
        return local_call(
            functools.partial(scan_kernel, which),
            jax.ShapeDtypeStruct((2, rows, 8 * HEAD), jnp.float32),
            "scan",
            COST["scan"],
            scratch=[work, work, work, pltpu.VMEM((STATES * 8, HEAD), jnp.float32), lanes, lanes],
            waits=waits,
        )(*packs, full, partner, smooth)

    def projected_out(which, *args):
        return local_call(
            functools.partial(output_kernel, which),
            (
                jax.ShapeDtypeStruct((rows, width), jnp.float32),
                jax.ShapeDtypeStruct((rows, width), jnp.bfloat16),
            ),
            "output",
            COST["output"],
            scratch=[pltpu.VMEM((2 * rows, 8 * HEAD), jnp.bfloat16)],
        )(*slots, *args)

    own_gate, sent_gate, pair_gate = gates
    far_keep, far_send = projected_out(
        1, scanned(1, [slots[i] for i in WAITS["scan"]]), pair_gate, pair_gate
    )
    far_sum = (far_keep + swap(far_send, near, count).astype(jnp.float32)).astype(jnp.bfloat16)
    from_far = swap(far_sum, far, count)
    near_keep, near_send = projected_out(0, scanned(0, [far_sum]), own_gate, sent_gate)
    from_near = swap(after(near_send, from_far), near, count)
    near_sum = near_keep + from_near.astype(jnp.float32) + from_far.astype(jnp.float32)
    return near_sum.astype(jnp.bfloat16)[None]


def solution(mesh):
    placed = (
        P("dp", "ctx", None),
        P("dp", "ctx", None),
        P("dp", "ctx", None),
        P("dp", "ctx", None),
        P(None, "dp"),
        P("dp"),
        P("dp", None),
        P(None, "dp"),
        P("dp"),
        P(None, "dp"),
        P("dp"),
        P("dp", None),
    )
    fits = mesh.shape["ctx"] == 1 and mesh.shape["dp"] == 32
    return jax.shard_map(
        grouped if fits else shards, mesh=mesh, in_specs=placed, out_specs=P("dp", "ctx", None), check_vma=False
    )
```

```python
import functools
import math

import jax
import jax.numpy as jnp
from jax import lax
from jax.experimental import pallas as pl
from jax.experimental.pallas import tpu as pltpu
from jax.sharding import PartitionSpec as P

HEAD_SIZE = 128


def shifted(value, axis, steps):
    count = lax.axis_size(axis)
    initial, last = (max(0, -steps), min(count, count - steps))
    return lax.ppermute(value, axis, [(source, source + steps) for source in range(initial, last)])


def entering(shard, axis, combine, identity):
    size, position = (lax.axis_size(axis), lax.axis_index(axis))
    everything = jax.tree.map(lambda part: lax.all_gather(part, axis), shard)
    start = jax.tree.map(
        lambda part, zero: jnp.broadcast_to(jnp.asarray(zero, part.dtype), part.shape),
        shard,
        identity,
    )

    def hop(k, before):
        reached = k < position
        new = combine(before, jax.tree.map(lambda part: part[k], everything))
        return jax.tree.map(lambda a, b: jnp.where(reached, a, b), new, before)

    return lax.fori_loop(0, size, hop, start)


def attend_whole(queries, keys_all, values_all, group):
    seq_len, kv_local, head_dim = keys_all.shape
    scale = 1.0 / math.sqrt(head_dim)
    block = min(512, seq_len)
    pieces = []
    for index in range(seq_len // block):
        begin = index * block
        end = begin + block
        query_block = queries[begin:end].reshape(block, kv_local, group, head_dim)
        scores = (
            jnp.einsum(
                "rgqd,ngd->gqrn", query_block, keys_all[:end], preferred_element_type=jnp.float32
            )
            * scale
        )
        visible = jnp.arange(end)[None, :] <= (begin + jnp.arange(block))[:, None]
        scores = jnp.where(visible, scores, -jnp.inf)
        top = jnp.max(scores, axis=-1, keepdims=True)
        raised = jnp.exp(scores - top)
        total = jnp.sum(raised, axis=-1)
        mixed = jnp.einsum(
            "gqrn,ngd->rgqd",
            raised.astype(jnp.bfloat16),
            values_all[:end],
            preferred_element_type=jnp.float32,
        )
        mixed = mixed / jnp.transpose(total, (2, 0, 1))[..., None]
        pieces.append(mixed.astype(jnp.bfloat16).reshape(block, kv_local, group * head_dim))
    return jnp.concatenate(pieces, axis=0)


def chain_pass(initial, step_size, drive_term, input_gain, readout, decay_rate):
    tok_rows = step_size.shape[0]
    block_len = math.gcd(tok_rows, 32)
    blocks = tok_rows // block_len

    def advance(state, inputs):
        size_block, drive_block, gain_block, read_block = inputs
        outputs = []
        for position in range(block_len):
            state = jnp.exp(size_block[position][None, :] * decay_rate) * state
            state = state + gain_block[position][:, None] * drive_block[position][None, :]
            outputs.append(jnp.dot(read_block[position], state, precision=lax.Precision.HIGHEST))
        return (state, jnp.stack(outputs))

    inputs = tuple(
        (
            item.reshape((blocks, block_len) + item.shape[1:])
            for item in (step_size, drive_term, input_gain, readout)
        )
    )
    final, outputs = lax.scan(advance, initial, inputs)
    return (final, outputs.reshape(tok_rows, -1))


def carried_part(carried, step_size, readout, decay_rate):
    tok_rows, channels = step_size.shape
    lower = (jnp.arange(tok_rows)[:, None] >= jnp.arange(tok_rows)[None, :]).astype(jnp.float32)
    cumulative = jnp.dot(lower, step_size, precision=lax.Precision.HIGHEST)
    block_len = math.gcd(tok_rows, 32)
    blocks = tok_rows // block_len
    cum_blocks = cumulative.reshape(blocks, block_len, channels)
    read_blocks = readout.reshape(blocks, block_len, readout.shape[1])

    def one_block(items):
        cum_block, read_block = items
        factor = jnp.exp(cum_block[:, None, :] * decay_rate[None])
        return jnp.sum(read_block[:, :, None] * factor * carried[None], axis=1)

    return lax.map(one_block, (cum_blocks, read_blocks)).reshape(tok_rows, channels)


def shards(
    query,
    key,
    value,
    gate_input,
    conv_weight,
    conv_bias,
    x_proj,
    dt_proj,
    dt_bias,
    a_log,
    d_skip,
    out_proj,
):
    tok_rows = query.shape[1]
    feature_width = query.shape[2]
    head_dim = HEAD_SIZE
    kv_heads = key.shape[2] // head_dim
    group = feature_width // key.shape[2]
    queries = query[0].reshape(tok_rows, kv_heads, group * head_dim)
    key_rows = key[0].reshape(tok_rows, kv_heads, head_dim)
    value_rows = value[0].reshape(tok_rows, kv_heads, head_dim)
    gathered_queries, gathered_keys, gathered_values = (
        lax.all_to_all(queries, "ctx", split_axis=1, concat_axis=0, tiled=True),
        lax.all_to_all(key_rows, "ctx", split_axis=1, concat_axis=0, tiled=True),
        lax.all_to_all(value_rows, "ctx", split_axis=1, concat_axis=0, tiled=True),
    )
    mixed = lax.all_to_all(
        attend_whole(gathered_queries, gathered_keys, gathered_values, group),
        "ctx",
        split_axis=0,
        concat_axis=1,
        tiled=True,
    )
    layer_input = mixed.reshape(tok_rows, feature_width)
    filter_taps, filter_bias, input_weight, step_weight, step_bias, decay_log, skip_gain = (
        lax.all_gather(conv_weight, "dp", axis=1, tiled=True),
        lax.all_gather(conv_bias, "dp", axis=0, tiled=True),
        lax.all_gather(x_proj, "dp", axis=0, tiled=True),
        lax.all_gather(dt_proj, "dp", axis=1, tiled=True),
        lax.all_gather(dt_bias, "dp", axis=0, tiled=True),
        lax.all_gather(a_log, "dp", axis=1, tiled=True),
        lax.all_gather(d_skip, "dp", axis=0, tiled=True),
    )
    taps = filter_taps.shape[0]
    earlier = shifted(layer_input[tok_rows - (taps - 1) :], "ctx", 1)
    padded = jnp.concatenate([earlier, layer_input], axis=0).astype(jnp.float32)
    filtered = filter_bias.astype(jnp.float32)[None, :]
    for tap in range(taps):
        filtered = (
            filtered + filter_taps[tap].astype(jnp.float32)[None, :] * padded[tap : tap + tok_rows]
        )
    smoothed = jax.nn.silu(filtered).astype(jnp.bfloat16)
    projected = jnp.dot(smoothed, input_weight, preferred_element_type=jnp.float32)
    rank = step_weight.shape[0]
    states = decay_log.shape[0]
    low_rank = projected[:, :rank]
    normed = (
        low_rank * lax.rsqrt(jnp.mean(low_rank * low_rank, axis=-1, keepdims=True) + 1e-06)
    ).astype(jnp.bfloat16)
    step_size = jax.nn.softplus(
        jnp.dot(normed, step_weight, preferred_element_type=jnp.float32)
        + step_bias.astype(jnp.float32)[None, :]
    )
    input_gain = projected[:, rank : rank + states]
    readout = projected[:, rank + states : rank + 2 * states]
    decay_rate = -jnp.exp(decay_log.astype(jnp.float32))
    smooth_float = smoothed.astype(jnp.float32)
    drive_term = step_size * smooth_float
    empty_state = jnp.zeros((states, feature_width), jnp.float32)
    end_state, local_out = chain_pass(
        empty_state, step_size, drive_term, input_gain, readout, decay_rate
    )
    total_decay = jnp.exp(decay_rate * jnp.sum(step_size, axis=0)[None, :])

    def combine(earlier_pair, later_pair):
        return (earlier_pair[0] * later_pair[0], later_pair[0] * earlier_pair[1] + later_pair[1])

    _, carried = entering(
        (total_decay, end_state),
        "ctx",
        combine,
        (jnp.ones_like(total_decay), jnp.zeros_like(end_state)),
    )
    carried_out = carried_part(carried, step_size, readout, decay_rate)
    scan_out = local_out + carried_out + skip_gain.astype(jnp.float32)[None, :] * smooth_float
    gated = (scan_out * jax.nn.silu(gate_input[0].astype(jnp.float32))).astype(jnp.bfloat16)
    piece = lax.all_gather(out_proj, "dp", axis=0, tiled=True)
    columns = lax.slice_in_dim(gated, 0, piece.shape[0], axis=1)
    result = jnp.zeros((tok_rows, out_proj.shape[1]), jnp.float32) + jnp.dot(
        columns, piece, preferred_element_type=jnp.float32
    )
    return result.astype(jnp.bfloat16)[None]


HEAD = HEAD_SIZE
RANK = 256
STATES = 16
TAPS = 4
EPS = 1e-06
LOG2E = 1.4426950408889634
GROUP = 4
MEMBERS = (1, 8)
SLOTS = (2, 4, 16)
COST = {"attention": 5, "project": 0, "combine": 0, "scan": 8, "output": 0}
WAITS = {"project": (4,), "add": (), "combine": (6,), "scan": ()}
XW, DT, AL, MISC, PACK_ROWS = 0, 288, 544, 560, 576


def swap(value, distance, count):
    return lax.ppermute(value, "dp", [(i, i ^ distance) for i in range(count)])


def local_call(kernel, out_shape, name, weight=0, scratch=(), waits=(), away=0):
    def call(*args):
        inside, anywhere = (pl.BlockSpec(memory_space=m) for m in (pltpu.VMEM, pl.ANY))
        return pl.pallas_call(
            kernel,
            out_shape=out_shape,
            in_specs=[anywhere] * away + [inside] * (len(args) - away) + [anywhere] * len(waits),
            out_specs=jax.tree.map(lambda _: inside, out_shape),
            scratch_shapes=list(scratch),
            name=name,
            cost_estimate=pl.CostEstimate(flops=1, bytes_accessed=weight * 3_690_000, transcendentals=0),
            compiler_params=pltpu.CompilerParams(vmem_limit_bytes=20 * 1024 * 1024),
        )(*args, *waits)

    return call


def placed(distance):
    member = sum(1 << k for k, bit in enumerate(MEMBERS) if distance & bit)
    return member, sum(1 << k for k, bit in enumerate(SLOTS) if distance & bit)


def after(value, *others):
    return lax.optimization_barrier((value,) + others)[0]


def attention_kernel(*refs):
    inputs, (own_ref, across_ref, send_ref) = refs[:3], refs[3:6]
    q_ref, k_ref, v_ref, arrived = refs[6:]
    copies = [
        pltpu.make_async_copy(source, held, arrived.at[n])
        for n, (source, held) in enumerate(zip(inputs, (q_ref, k_ref, v_ref)))
    ]
    for copy in copies:
        copy.start()
    position = lax.axis_index("dp")
    rows = q_ref.shape[0]
    scale = 1.0 / math.sqrt(HEAD)
    row = lax.broadcasted_iota(jnp.int32, (GROUP, rows, rows), 1).reshape(GROUP * rows, rows)
    col = lax.broadcasted_iota(jnp.int32, (GROUP * rows, rows), 1)
    visible = col <= row
    for copy in copies:
        copy.wait()

    def lanes(index):
        return pl.ds(pl.multiple_of(index * HEAD, HEAD), HEAD)

    for pair in range(8):
        kv = (position // 4) ^ pair
        heads = [position ^ (pair * 4 + inner) for inner in range(4)]
        stacked = jnp.concatenate([q_ref[:, lanes(h)] for h in heads], axis=0)
        keys = k_ref[:, lanes(kv)]
        values = v_ref[:, lanes(kv)]
        scores = lax.dot_general(
            stacked, keys, (((1,), (1,)), ((), ())), preferred_element_type=jnp.float32
        )
        scores = jnp.where(visible, scores * scale, -jnp.inf)
        top = jnp.max(scores, axis=-1, keepdims=True)
        raised = jnp.exp(scores - top)
        total = jnp.sum(raised, axis=-1, keepdims=True)
        mixed = jnp.dot(raised.astype(jnp.bfloat16), values, preferred_element_type=jnp.float32)
        mixed = (mixed / total).astype(jnp.bfloat16)
        for inner in range(4):
            j, slot = placed(pair * 4 + inner)
            here = slice(slot * HEAD, (slot + 1) * HEAD)
            target = (own_ref, send_ref.at[0], across_ref, send_ref.at[1])[j]
            target[:, here] = mixed[inner * rows : (inner + 1) * rows]


def gates_kernel(g_ref, own_ref, across_ref, send_ref):
    position = lax.axis_index("dp")
    for distance in range(32):
        j, slot = placed(distance)
        here = slice(slot * HEAD, (slot + 1) * HEAD)
        head = position ^ distance
        target = (own_ref, send_ref.at[0], across_ref, send_ref.at[1])[j]
        target[:, here] = g_ref[:, pl.ds(pl.multiple_of(head * HEAD, HEAD), HEAD)]


def slot_packs(refs):
    own, z_ref, x_ref, y_ref, xy_ref, xyz_ref = refs
    return [
        own,
        x_ref.at[:PACK_ROWS],
        y_ref.at[:PACK_ROWS],
        xy_ref,
        z_ref,
        x_ref.at[PACK_ROWS:],
        y_ref.at[PACK_ROWS:],
        xyz_ref,
    ]


def project_kernel(*refs):
    packs = slot_packs(refs[:6])
    own_ref, send_ref, pair_ref = refs[6:9]
    smooth_ref, pkeep_ref, psend_ref, weight_ref = refs[-4:]
    sources = [own_ref, send_ref.at[0], pair_ref.at[0], pair_ref.at[1]]
    rows = own_ref.shape[0]
    row = lax.broadcasted_iota(jnp.int32, (rows, HEAD), 0)
    masks = [row >= k for k in range(TAPS)]
    for slot in range(8):
        here = slice(slot * HEAD, (slot + 1) * HEAD)
        weight_ref[:, here] = packs[slot][XW : XW + 288, :]
        misc = packs[slot][MISC : MISC + 16, :].astype(jnp.float32)
        for j in range(GROUP):
            mixed = sources[j][:, here].astype(jnp.float32)
            filtered = misc[4:5] + jnp.zeros_like(mixed)
            for tap in range(TAPS):
                shift = TAPS - 1 - tap
                moved = mixed
                if shift:
                    moved = jnp.where(masks[shift], pltpu.roll(mixed, shift, 0), 0.0)
                filtered = filtered + misc[tap : tap + 1] * moved
            smooth = filtered / (1.0 + jnp.exp(-filtered))
            smooth_ref[j, :, here] = smooth.astype(jnp.bfloat16)
    for j in range(GROUP):
        part = lax.dot_general(
            smooth_ref[j],
            weight_ref[...],
            (((1,), (1,)), ((), ())),
            preferred_element_type=jnp.float32,
        )
        target = psend_ref if j % 2 else pkeep_ref
        half = j // 2
        target[:, half * 256 : half * 256 + 256] = part[:, :256]
        target[:, 512 + half * 32 : 512 + half * 32 + 32] = part[:, 256:288]


def join_kernel(a_ref, b_ref, *rest):
    out_ref = rest[-1]
    out_ref[:PACK_ROWS] = a_ref[...]
    out_ref[PACK_ROWS:] = b_ref[...]


def add_kernel(a_ref, b_ref, *rest):
    rest[-1][...] = a_ref[...] + b_ref[...]


def combine_kernel(chip_ref, other_ref, *rest):
    full_ref = rest[-1]
    full_ref[:, :256] = chip_ref[:, :256] + other_ref[:, 256:512]
    full_ref[:, 256:512] = chip_ref[:, 256:512] + other_ref[:, :256]
    lanes = lax.broadcasted_iota(jnp.int32, (chip_ref.shape[0], HEAD), 1)
    other = other_ref[:, 512:]
    turned = jnp.where(lanes < 32, pltpu.roll(other, HEAD - 32, 1), pltpu.roll(other, 32, 1))
    full_ref[:, 512:] = chip_ref[:, 512:] + turned


def scan_kernel(half, *refs):
    packs, (f0_ref, f1_ref, smooth_ref) = slot_packs(refs[:6]), refs[6:9]
    scanned_ref, size_ref, drive_ref, out_ref, rate_ref, gain_ref, read_ref = refs[-7:]
    rows = f0_ref.shape[0]
    sources = [f0_ref, f1_ref]
    for s in range(2):
        low = sources[s][:, half * 256 : half * 256 + 256]
        normed = low * lax.rsqrt(jnp.mean(low * low, axis=-1, keepdims=True) + EPS)
        normed = normed.astype(jnp.bfloat16)
        both = sources[s][:, 512 + half * 32 : 512 + half * 32 + 32]
        for n in range(STATES):
            wide = jnp.broadcast_to(both[:, n : n + 1], (rows, HEAD))
            gain_ref[s, pl.ds(n, rows, stride=STATES), :] = wide
            wide = jnp.broadcast_to(both[:, STATES + n : STATES + n + 1], (rows, HEAD))
            read_ref[s, pl.ds(n, rows, stride=STATES), :] = wide
        for slot in range(8):
            bias = packs[slot][MISC : MISC + 16, :].astype(jnp.float32)[5:6]
            raw = (
                jnp.dot(
                    normed, packs[slot][DT : DT + RANK, :], preferred_element_type=jnp.float32
                )
                + bias
            )
            size = jnp.maximum(raw, 0.0) + jnp.log1p(jnp.exp(-jnp.abs(raw)))
            smooth = smooth_ref[2 * half + s, :, slot * HEAD : (slot + 1) * HEAD]
            size_ref[s, pl.ds(slot, rows, stride=8), :] = size
            drive_ref[s, pl.ds(slot, rows, stride=8), :] = size * smooth.astype(jnp.float32)
    for slot in range(8):
        rate = -jnp.exp(packs[slot][AL : AL + STATES, :].astype(jnp.float32)) * LOG2E
        rate_ref[pl.ds(slot, STATES, stride=8), :] = rate

    def one(t, states):
        new = []
        for s in range(2):
            at = pl.ds(pl.multiple_of(t * 8, 8), 8)
            size = size_ref[s, at, :]
            drive = drive_ref[s, at, :]
            total = [None, None]
            for n in range(STATES):
                decay = jnp.exp2(size * rate_ref[n * 8 : n * 8 + 8, :])
                gain = gain_ref[s, pl.ds(t * STATES + n, 1), :]
                read = read_ref[s, pl.ds(t * STATES + n, 1), :]
                state = decay * states[s * STATES + n] + gain * drive
                new.append(state)
                term = read * state
                total[n % 2] = term if total[n % 2] is None else total[n % 2] + term
            out_ref[s, at, :] = total[0] + total[1]
        return tuple(new)

    zero = jnp.zeros((8, HEAD), jnp.float32)
    lax.fori_loop(0, rows, one, (zero,) * (2 * STATES), unroll=2)
    for s in range(2):
        for slot in range(8):
            here = slice(slot * HEAD, (slot + 1) * HEAD)
            skip = packs[slot][MISC : MISC + 16, :].astype(jnp.float32)[6:7]
            smooth = smooth_ref[2 * half + s, :, here].astype(jnp.float32)
            scanned = out_ref[s, pl.ds(slot, rows, stride=8), :] + skip * smooth
            scanned_ref[s, :, here] = scanned


def output_kernel(half, *refs):
    slots = refs[:-6]
    scanned_ref, g0_ref, g1_ref, keep_ref, send_ref, gated_ref = refs[-6:]
    rows = keep_ref.shape[0]
    gates = [g0_ref.at[0] if half else g0_ref, g1_ref.at[half]]
    for s in range(2):
        for slot in range(8):
            here = slice(slot * HEAD, (slot + 1) * HEAD)
            gate = gates[s][:, here].astype(jnp.float32)
            gated = scanned_ref[s, :, here] * (gate / (1.0 + jnp.exp(-gate)))
            gated_ref[s * rows : (s + 1) * rows, here] = gated.astype(jnp.bfloat16)
    width = 512
    for begin in range(0, keep_ref.shape[1], width):
        columns = slice(begin, begin + width)
        weight = jnp.concatenate([slot[:, columns] for slot in slots], axis=0)
        total = jnp.dot(gated_ref[...], weight, preferred_element_type=jnp.float32)
        keep_ref[:, columns] = total[:rows]
        send_ref[:, columns] = total[rows:].astype(send_ref.dtype)


def grouped(query, key, value, gate_input, conv_weight, conv_bias, x_proj, dt_proj, dt_bias, a_log, d_skip, out_proj):
    count = lax.axis_size("dp")
    rows = query.shape[1]
    width = out_proj.shape[1]
    pack = jnp.concatenate(
        [
            x_proj.T,
            dt_proj,
            a_log,
            conv_weight,
            conv_bias[None],
            dt_bias[None],
            d_skip[None],
            jnp.zeros((PACK_ROWS - MISC - 7, HEAD), jnp.bfloat16),
        ],
        axis=0,
    )

    near, far = MEMBERS
    bit_x, bit_y, bit_z = SLOTS

    quarter = jax.ShapeDtypeStruct((rows, 8 * HEAD), jnp.bfloat16)
    both = jax.ShapeDtypeStruct((2, rows, 8 * HEAD), jnp.bfloat16)

    def spread(own, across, send):
        arrived = swap(send, near, count)
        pair = swap(jnp.stack([across, arrived[1]]), far, count)
        return own, arrived, pair

    made = local_call(
        attention_kernel,
        (quarter, quarter, both),
        "attention",
        COST["attention"],
        scratch=[
            pltpu.VMEM(query.shape[1:], jnp.bfloat16),
            pltpu.VMEM(key.shape[1:], jnp.bfloat16),
            pltpu.VMEM(value.shape[1:], jnp.bfloat16),
            pltpu.SemaphoreType.DMA((3,)),
        ],
        away=3,
    )(query[0], key[0], value[0])
    mixed = spread(*made)
    pack_z = swap(pack, bit_z, count)
    slot_x = swap(after(out_proj, pack), bit_x, count)
    slot_y = swap(after(out_proj, pack), bit_y, count)
    pack_two = local_call(join_kernel, jax.ShapeDtypeStruct((2 * PACK_ROWS, HEAD), jnp.bfloat16), "join", waits=[slot_x, slot_y])(pack, pack_z)
    pack_x = swap(pack_two, bit_x, count)
    pack_y = swap(pack_two, bit_y, count)
    pack_xy = swap(pack_y[:PACK_ROWS], bit_x, count)
    pack_xyz = swap(pack_x[PACK_ROWS:], bit_y, count)
    packs = [pack, pack_z, pack_x, pack_y, pack_xy, pack_xyz]
    slot_xy = swap(slot_y, bit_x, count)
    slot_z = swap(after(out_proj, mixed[1]), bit_z, count)
    slot_zx = swap(slot_z, bit_x, count)
    slot_zy = swap(slot_z, bit_y, count)
    slot_zxy = swap(slot_zx, bit_y, count)
    slots = [out_proj, slot_x, slot_y, slot_xy, slot_z, slot_zx, slot_zy, slot_zxy]

    wide = jax.ShapeDtypeStruct((rows, 640), jnp.float32)
    smooth, pkeep, psend = local_call(
        project_kernel,
        (jax.ShapeDtypeStruct((GROUP, rows, 8 * HEAD), jnp.bfloat16), wide, wide),
        "project",
        COST["project"],
        scratch=[pltpu.VMEM((288, 8 * HEAD), jnp.bfloat16)],
        waits=[slots[i] for i in WAITS["project"]],
    )(*packs, *mixed)
    chip = local_call(
        add_kernel, wide, "add", waits=[slots[i] for i in WAITS["add"]]
    )(pkeep, swap(psend, near, count))
    full = local_call(
        combine_kernel, wide, "combine", COST["combine"], waits=[slots[i] for i in WAITS["combine"]]
    )(chip, swap(chip, far, count))
    partner = swap(full, near, count)
    gate_source = after(gate_input[0], chip)
    gates = spread(*local_call(gates_kernel, (quarter, quarter, both), "gates")(gate_source))

    def scanned(which, waits):
        work = pltpu.VMEM((2, rows * 8, HEAD), jnp.float32)
        lanes = pltpu.VMEM((2, rows * STATES, HEAD), jnp.float32)
        return local_call(
            functools.partial(scan_kernel, which),
            jax.ShapeDtypeStruct((2, rows, 8 * HEAD), jnp.float32),
            "scan",
            COST["scan"],
            scratch=[work, work, work, pltpu.VMEM((STATES * 8, HEAD), jnp.float32), lanes, lanes],
            waits=waits,
        )(*packs, full, partner, smooth)

    def projected_out(which, *args):
        return local_call(
            functools.partial(output_kernel, which),
            (
                jax.ShapeDtypeStruct((rows, width), jnp.float32),
                jax.ShapeDtypeStruct((rows, width), jnp.bfloat16),
            ),
            "output",
            COST["output"],
            scratch=[pltpu.VMEM((2 * rows, 8 * HEAD), jnp.bfloat16)],
        )(*slots, *args)

    own_gate, sent_gate, pair_gate = gates
    far_keep, far_send = projected_out(
        1, scanned(1, [slots[i] for i in WAITS["scan"]]), pair_gate, pair_gate
    )
    far_sum = (far_keep + swap(far_send, near, count).astype(jnp.float32)).astype(jnp.bfloat16)
    from_far = swap(far_sum, far, count)
    near_keep, near_send = projected_out(0, scanned(0, [far_sum]), own_gate, sent_gate)
    from_near = swap(after(near_send, from_far), near, count)
    near_sum = near_keep + from_near.astype(jnp.float32) + from_far.astype(jnp.float32)
    return near_sum.astype(jnp.bfloat16)[None]


def solution(mesh):
    placed = (
        P("dp", "ctx", None),
        P("dp", "ctx", None),
        P("dp", "ctx", None),
        P("dp", "ctx", None),
        P(None, "dp"),
        P("dp"),
        P("dp", None),
        P(None, "dp"),
        P("dp"),
        P(None, "dp"),
        P("dp"),
        P("dp", None),
    )
    fits = mesh.shape["ctx"] == 1 and mesh.shape["dp"] == 32
    return jax.shard_map(
        grouped if fits else shards, mesh=mesh, in_specs=placed, out_specs=P("dp", "ctx", None), check_vma=False
    )
```
